128 devices in a mesh: section: 4 (over y_lo, core), dp: 4 (over z), node: 8 (over y_hi, x).
Axes of the slice: x: 4, y: 4 (y_hi: 2, y_lo: 2; y = y_hi * 2 + y_lo), z: 4, core: 2. Of those that a mesh axis runs over, the one named last changes fastest.
Arguments:
- grad_out: bfloat16 [2, 256, 3072], P(None, ('dp', 'node')), may hold values from -6 to 6
- layer_in: bfloat16 [4, 2, 256, 3072], P('section', None, ('dp', 'node')), may hold values from -6 to 6
- gate_pre: bfloat16 [4, 2, 256, 8192], P('section', None, 'dp', 'node'), may hold values from -6 to 6
- up_pre: bfloat16 [4, 2, 256, 8192], P('section', None, 'dp', 'node'), may hold values from -6 to 6
- expert_ids: int32 [4, 2, 256, 2], P('section', None, 'dp'), may hold values from 0 to 7, as said below
- route_weight: float32 [4, 2, 256, 2], P('section', None, 'dp'), may hold values from 0.3 to 1
- w_gate: bfloat16 [4, 3072, 8192], P('section', None, 'node'), may hold values from -0.109375 to 0.109375
- w_up: bfloat16 [4, 3072, 8192], P('section', None, 'node'), may hold values from -0.109375 to 0.109375
- w_down: bfloat16 [4, 8192, 3072], P('section', 'node'), may hold values from -0.0625 to 0.0625
Outputs:
- grad_in: bfloat16 [4, 2, 256, 3072], P('section', None, ('dp', 'node'))
- grad_gate_w: bfloat16 [4, 3072, 8192], P('section', 'dp', 'node')
- grad_up_w: bfloat16 [4, 3072, 8192], P('section', 'dp', 'node')
- grad_down_w: bfloat16 [4, 8192, 3072], P('section', 'node', 'dp')
The draws below stay inside these ranges and needn't reach their ends.
Inputs may be any that keep to these rules, and one draw needn't show every extreme that they name: `expert_ids`: each token names 2 different experts.
All inputs are finite; a program needn't handle non-finite values.
Results may differ from the reference program's by a relative error of at most 0.025.
Values may be sent and summed in bfloat16 or wider, within the bound.
A program may use at most 192 MiB of HBM per device.

```python
import jax
import jax.numpy as jnp
from jax import lax

D = 3072
EXPERTS = 8
HID = 8192
TOPK = 2
MICRO = 2
MB = 256
SECTIONS = 4
N_DP = 4


def draw_expert_ids(key, part):
    key = jax.random.fold_in(key, 7)
    key_other, key_zero, key_second, key_flip = jax.random.split(key, 4)
    shape = (SECTIONS, MICRO, MB)
    other = jax.random.randint(key_other, shape, 1, EXPERTS)
    to_zero = jax.random.randint(key_zero, shape, 0, 8) < 7
    first = jnp.where(to_zero, 0, other)
    second = (first + jax.random.randint(key_second, shape, 1, EXPERTS)) % EXPERTS
    flipped = jax.random.randint(key_flip, shape, 0, 2) == 1
    column_a = jnp.where(flipped, second, first)
    column_b = jnp.where(flipped, first, second)
    return jnp.stack([column_a, column_b], axis=-1).astype(jnp.int32)


def steps_of(rng, dims, cuts, smallest, high):
    loudness = 1.0
    for position, shards_of in cuts:
        draws = jax.random.uniform(jax.random.fold_in(jax.random.fold_in(rng, 6), position), (shards_of,), jnp.float32, smallest / len(cuts), high / len(cuts))
        loudness = loudness * jnp.repeat(jnp.exp(draws), dims[position] // shards_of).reshape((-1,) + (1,) * (len(dims) - 1 - position))
    return loudness


def centred(own_key, shape, width, reach, cuts=(), kind=jnp.bfloat16):
    result = jax.random.normal(own_key, shape, jnp.float32) * width
    if len(cuts) > 0:
        result = steps_of(own_key, shape, cuts, -0.22, 0.18) * result
    return jnp.clip(result, min=-reach, max=reach).astype(kind)


def setup_inputs(seed: int = 0) -> dict:
    seeds = jax.random.split(jax.random.key(seed), 10)
    return {
        "grad_out": centred(seeds[0], (MICRO, MB, D), 1.0, 6.0, ((1, 32),)),
        "layer_in": centred(seeds[1], (SECTIONS, MICRO, MB, D), 1.0, 6.0, ((0, 4), (2, 32))),
        "gate_pre": centred(seeds[2], (SECTIONS, MICRO, MB, HID), 1.5, 6.0, ((0, 4), (2, 4), (3, 8))),
        "up_pre": centred(seeds[3], (SECTIONS, MICRO, MB, HID), 1.0, 6.0, ((0, 4), (2, 4), (3, 8))),
        "expert_ids": draw_expert_ids(jax.random.fold_in(seeds[9], 71), 0),
        "route_weight": jnp.clip(0.3 + 0.7 * jax.random.uniform(seeds[5], (SECTIONS, MICRO, MB, TOPK), jnp.float32) ** steps_of(seeds[5], (SECTIONS, MICRO, MB, TOPK), ((0, 4), (2, 4)), -0.2, 0.2), 0.3, 1.0),
        "w_gate": centred(seeds[6], (SECTIONS, D, HID), D ** -0.5, 0.109375, ((0, 4), (2, 8))),
        "w_up": centred(seeds[7], (SECTIONS, D, HID), D ** -0.5, 0.109375, ((0, 4), (2, 8))),
        "w_down": centred(seeds[8], (SECTIONS, HID, D), HID ** -0.5, 0.0625, ((0, 4), (1, 8))),
    }


def reference(grad_out, layer_in, gate_pre, up_pre, expert_ids, route_weight, w_gate, w_up, w_down):
    layers = layer_in.shape[0]
    micro = layer_in.shape[1]
    total = layer_in.shape[2]
    size = total // N_DP
    carried = [grad_out[index] for index in range(micro)]
    grad_in = [None] * layers
    gate_list = [None] * layers
    up_list = [None] * layers
    down_list = [None] * layers
    for level in reversed(range(layers)):
        results = []
        saved = []
        for index in range(micro):
            upstream = carried[index]
            gate = gate_pre[level, index].astype(jnp.float32)
            upval = up_pre[level, index].astype(jnp.float32)
            coef = jnp.sum(jnp.where(expert_ids[level, index] == 0, route_weight[level, index], jnp.float32(0.0)), axis=-1)[:, None]
            back = jnp.dot(upstream, w_down[level].T, preferred_element_type=jnp.float32) * coef
            sigma = jax.nn.sigmoid(gate)
            active = gate * sigma
            d_gate = (back * upval * sigma * (1.0 + gate * (1.0 - sigma))).astype(jnp.bfloat16)
            d_up = (back * active).astype(jnp.bfloat16)
            hidden = (coef * active * upval).astype(jnp.bfloat16)
            saved.append((upstream, d_gate, d_up, hidden))
            summed = upstream.astype(jnp.float32) + jnp.dot(d_gate, w_gate[level].T, preferred_element_type=jnp.float32) + jnp.dot(d_up, w_up[level].T, preferred_element_type=jnp.float32)
            outcome = summed.astype(jnp.bfloat16)
            carried[index] = outcome
            results.append(outcome)
        grad_in[level] = jnp.stack(results)
        total_gate = jnp.zeros((D, HID), jnp.float32)
        total_up = jnp.zeros((D, HID), jnp.float32)
        total_down = jnp.zeros((HID, D), jnp.float32)
        for replica in range(N_DP):
            start = replica * size
            part_gate = jnp.zeros((D, HID), jnp.float32)
            part_up = jnp.zeros((D, HID), jnp.float32)
            part_down = jnp.zeros((HID, D), jnp.float32)
            for index in range(micro):
                upstream, d_gate, d_up, hidden = saved[index]
                inputs = layer_in[level, index, start:start + size]
                part_gate = part_gate + jnp.dot(inputs.T, d_gate[start:start + size], preferred_element_type=jnp.float32)
                part_up = part_up + jnp.dot(inputs.T, d_up[start:start + size], preferred_element_type=jnp.float32)
                part_down = part_down + jnp.dot(hidden[start:start + size].T, upstream[start:start + size], preferred_element_type=jnp.float32)
            total_gate = total_gate + lax.optimization_barrier(part_gate.astype(jnp.bfloat16)).astype(jnp.float32)
            total_up = total_up + lax.optimization_barrier(part_up.astype(jnp.bfloat16)).astype(jnp.float32)
            total_down = total_down + lax.optimization_barrier(part_down.astype(jnp.bfloat16)).astype(jnp.float32)
        gate_list[level] = total_gate.astype(jnp.bfloat16)
        up_list[level] = total_up.astype(jnp.bfloat16)
        down_list[level] = total_down.astype(jnp.bfloat16)
    return (jnp.stack(grad_in), jnp.stack(gate_list), jnp.stack(up_list), jnp.stack(down_list))
```

```python
import jax
import jax.numpy as jnp
from jax import lax
from jax.experimental import pallas as pl
from jax.experimental.pallas import tpu as pltpu
from jax.sharding import PartitionSpec as P

MESH = pl.DeviceIdType.MESH
F32 = jnp.float32
BF16 = jnp.bfloat16
SECTIONS = 4
DP = 4
NODES = 8
MICRO = 2
OWN = 8
ROWS = OWN * NODES
ALL = ROWS * DP
WIDTH = 3072
HID = 1024
CB = WIDTH // NODES
DB = WIDTH // DP
WD_SLOTS = 4
WG_SLOTS = 6
OFFSETS = ((1, 2), (1, 1), (1, 3), (0, 2), (1, 0), (0, 1), (0, 3))


def near(n, offset):
    high, x = lax.div(n, 4), lax.rem(n, 4)
    return lax.rem(high + offset[0], 2) * 4 + lax.rem(x + offset[1], 4)


def dot(a, b):
    return lax.dot_general(a, b, (((1,), (0,)), ((), ())), preferred_element_type=F32)


def remote(src, dst, send, recv, **device):
    return pltpu.make_async_remote_copy(
        src_ref=src,
        dst_ref=dst,
        send_sem=send,
        recv_sem=recv,
        device_id=device,
        device_id_type=MESH,
    )


def body(
    grad_out, layer_in, gate_pre, up_pre, ids, route, w_gate, w_up, w_down,
    grad_in, g_gate, g_up, g_down,
    wd_raw, wg_raw, wdt, wgut,
    ids_v, route_v, lin_v, coef_v,
    go, dyg, prt, snd, dgu,
    gates, ups, backs, dys, dys_send,
    lsc, lx, lg, lin_t, hid_t, dga, dua,
    acc_g, acc_u, acc_d, out_g, out_u, out_d,
    ret, gi, fp, fs, fr,
    s_small, s_wd, s_wg, s_out,
    ss_go, rs_go, ss_sc, rs_sc, ss_ga, rs_ga,
    ss_gate, rs_gate, ss_up, rs_up, ss_lx, rs_lx, ss_lg, rs_lg,
    ss_b, rs_b, ss_dy, rs_dy, ss_ret, rs_ret, ss_f, rs_f,
):
    s = lax.axis_index("section")
    r = lax.axis_index("dp")
    n = lax.axis_index("node")
    above = lax.rem(s + 1, SECTIONS)
    below = lax.rem(s + SECTIONS - 1, SECTIONS)
    own_rows = pl.ds(pl.multiple_of(r * ROWS, ROWS), ROWS)

    def peer(k):
        return lax.rem(r + k, DP)

    barrier = pltpu.get_barrier_semaphore()
    for offset in OFFSETS:
        pl.semaphore_signal(
            barrier, inc=1, device_id={"node": near(n, offset)}, device_id_type=MESH
        )
    for k in range(1, DP):
        pl.semaphore_signal(barrier, inc=1, device_id={"dp": peer(k)}, device_id_type=MESH)

    @pl.when(s < SECTIONS - 1)
    def _():
        for j in range(NODES):
            pl.semaphore_signal(
                barrier, inc=1, device_id={"section": above, "node": j}, device_id_type=MESH
            )

    @pl.when(s > 0)
    def _():
        for j in range(NODES):
            pl.semaphore_signal(
                barrier, inc=1, device_id={"section": below, "node": j}, device_id_type=MESH
            )

    def load_wd(j):
        return pltpu.make_async_copy(
            w_down.at[:, pl.ds(j * CB, CB)], wd_raw.at[j % WD_SLOTS], s_wd.at[j]
        )

    def load_wg(j):
        ref = w_gate if j < NODES else w_up
        return pltpu.make_async_copy(
            ref.at[pl.ds((j % NODES) * CB, CB), :], wg_raw.at[j % WG_SLOTS], s_wg.at[j]
        )

    for j in range(WD_SLOTS):
        load_wd(j).start()
    small = [
        pltpu.make_async_copy(ids, ids_v, s_small.at[0]),
        pltpu.make_async_copy(route, route_v, s_small.at[1]),
        pltpu.make_async_copy(layer_in, lin_v, s_small.at[2]),
        pltpu.make_async_copy(gate_pre, gates.at[:, own_rows, :], s_small.at[3]),
        pltpu.make_async_copy(up_pre, ups.at[:, own_rows, :], s_small.at[4]),
        pltpu.make_async_copy(grad_out, go.at[n], s_small.at[5]),
    ]
    for copy in small:
        copy.start()
    for j in range(WG_SLOTS):
        load_wg(j).start()

    neighbours = jnp.minimum(s, 1) + jnp.minimum(SECTIONS - 1 - s, 1)
    pl.semaphore_wait(barrier, NODES - 1 + DP - 1 + neighbours * NODES)

    def send_go(q):
        return remote(
            grad_out, go.at[n], ss_go.at[q], rs_go.at[n], node=near(n, OFFSETS[q])
        )

    def send_gate(k):
        return remote(
            gate_pre, gates.at[:, own_rows, :], ss_gate.at[k], rs_gate.at[r], dp=peer(k)
        )

    def send_up(k):
        return remote(
            up_pre, ups.at[:, own_rows, :], ss_up.at[k], rs_up.at[r], dp=peer(k)
        )

    def send_lx(k):
        return remote(
            lsc.at[peer(k)], lx.at[r], ss_lx.at[k], rs_lx.at[r], dp=peer(k)
        )

    def send_lg(q):
        return remote(lx, lg.at[n], ss_lg.at[q], rs_lg.at[n], node=near(n, OFFSETS[q]))

    @pl.when(s == SECTIONS - 1)
    def _():
        for q in range(NODES - 1):
            send_go(q).start()

    for copy in small:
        copy.wait()
    diagonal = lax.broadcasted_iota(jnp.int32, (ROWS, ROWS), 0) == lax.broadcasted_iota(
        jnp.int32, (ROWS, ROWS), 1
    )
    for m in range(MICRO):
        across = jnp.sum(
            jnp.where(ids_v[m] == 0, route_v[m], jnp.float32(0.0)), axis=0, keepdims=True
        )
        coef_v[m * ROWS : (m + 1) * ROWS, :] = jnp.sum(
            jnp.where(diagonal, across, jnp.float32(0.0)), axis=1, keepdims=True
        )

    def exchange():
        scale = jnp.concatenate(
            [
                coef_v[pl.ds(pl.multiple_of(m * ROWS + n * OWN, OWN), OWN), :]
                for m in range(MICRO)
            ],
            axis=0,
        )
        for j in range(DP):
            lsc[j] = (lin_v[:, j * DB : (j + 1) * DB].astype(F32) * scale).astype(BF16)
        lx[r] = lsc[r]
        for k in range(1, DP):
            send_lx(k).start()
        for k in range(1, DP):
            send_gate(k).start()
        for k in range(1, DP):
            send_up(k).start()

    def gather_inputs():
        for k in range(1, DP):
            remote(lsc.at[0], lx.at[peer(k)], ss_lx.at[k], rs_lx.at[peer(k)], dp=peer(k)).wait_recv()
        for q in range(NODES - 1):
            send_lg(q).start()
        lg[n] = lx[...]

    def prepare():
        for offset in OFFSETS:
            j = near(n, offset)
            remote(lx, lg.at[j], ss_lg.at[0], rs_lg.at[j], node=j).wait_recv()
        for m in range(MICRO):
            rows = jnp.concatenate(
                [
                    lg[i, k, :, :].astype(F32)[m * OWN : (m + 1) * OWN]
                    for k in range(DP)
                    for i in range(NODES)
                ],
                axis=0,
            )
            lin_t[m] = rows.astype(BF16).T
        for k in range(1, DP):
            j = peer(k)
            rows = pl.ds(pl.multiple_of(j * ROWS, ROWS), ROWS)
            remote(gate_pre, gates.at[:, rows, :], ss_gate.at[k], rs_gate.at[j], dp=j).wait_recv()
            remote(up_pre, ups.at[:, rows, :], ss_up.at[k], rs_up.at[j], dp=j).wait_recv()
        for m in range(MICRO):
            for c in range(2):
                rows = pl.ds(c * 128, 128)
                g = gates[m, rows, :].astype(F32)
                hidden = (g * jax.nn.sigmoid(g) * ups[m, rows, :].astype(F32)).astype(BF16)
                hid_t[m, :, c * 128 : (c + 1) * 128] = hidden.T

    @pl.when(s < 2)
    def _():
        exchange()

    for j in range(NODES):
        load_wd(j).wait()
        wdt[j] = wd_raw[j % WD_SLOTS].T
        if j + WD_SLOTS < NODES:
            load_wd(j + WD_SLOTS).start()
    for j in range(2 * NODES):
        load_wg(j).wait()
        half = (j // NODES) * HID
        wgut[j % NODES, half : half + HID, :] = wg_raw[j % WG_SLOTS].T
        if j + WG_SLOTS < 2 * NODES:
            load_wg(j + WG_SLOTS).start()

    @pl.when(s < 2)
    def _():
        gather_inputs()
        prepare()

    def send_ga(m, q):
        return remote(
            dyg.at[m, n], dyg.at[m, n], ss_ga.at[m, q], rs_ga.at[m, n], node=near(n, OFFSETS[q])
        )

    def recv_ga(m, j):
        return remote(dyg.at[m, j], dyg.at[m, j], ss_ga.at[m, 0], rs_ga.at[m, j], node=j)

    @pl.when(s == SECTIONS - 1)
    def _():
        for offset in OFFSETS:
            j = near(n, offset)
            remote(grad_out, go.at[j], ss_go.at[0], rs_go.at[j], node=j).wait_recv()
        for j in range(NODES):
            block = go[:, :, j * CB : (j + 1) * CB].astype(F32)
            for m in range(MICRO):
                dyg[m, j] = (
                    block[:, m * OWN : (m + 1) * OWN, :].reshape(ROWS, CB).astype(BF16)
                )

    @pl.when(s < SECTIONS - 1)
    def _():
        for m in range(MICRO):
            total = jnp.zeros((ROWS, CB), F32)
            for j in range(NODES):
                remote(
                    snd.at[m, j], prt.at[m, j], ss_sc.at[m, j], rs_sc.at[m, j],
                    section=above, node=j,
                ).wait_recv()
                total = total + prt[m, j].astype(F32)
            dyg[m, n] = total.astype(BF16)
            for q in range(NODES - 1):
                send_ga(m, q).start()

    def send_sc(m, j):
        return remote(
            snd.at[m, j], prt.at[m, n], ss_sc.at[m, j], rs_sc.at[m, n], section=below, node=j
        )

    def send_b(m, k):
        return remote(
            backs.at[m, own_rows, :], backs.at[m, own_rows, :],
            ss_b.at[m, k], rs_b.at[m, r], dp=peer(k),
        )

    def send_dy(m, k):
        return remote(
            dys_send.at[m, k - 1], dys.at[m, :, own_rows, :],
            ss_dy.at[m, k], rs_dy.at[m, r], dp=peer(k),
        )

    def send_f(m, q):
        return remote(
            fs.at[m, q], fr.at[m, n], ss_f.at[m, q], rs_f.at[m, n], node=near(n, OFFSETS[q])
        )

    for m in range(MICRO):
        back = dot(dyg[m, n], wdt[n])
        for offset in OFFSETS[::-1]:
            j = near(n, offset)

            @pl.when(s < SECTIONS - 1)
            def _(j=j):
                recv_ga(m, j).wait_recv()

            back = back + dot(dyg[m, j], wdt[j])
        backs[m, own_rows, :] = back.astype(BF16)
        for k in range(1, DP):
            send_b(m, k).start()
        back = back * coef_v[m * ROWS : (m + 1) * ROWS, :]
        gate = gates[m, own_rows, :].astype(F32)
        sigma = jax.nn.sigmoid(gate)
        dgu[m, :, :HID] = (
            back * ups[m, own_rows, :].astype(F32) * sigma * (1.0 + gate * (1.0 - sigma))
        ).astype(BF16)
        dgu[m, :, HID:] = (back * gate * sigma).astype(BF16)
        for offset in OFFSETS + ((0, 0),):
            j = near(n, offset)
            part = dot(dgu[m], wgut[j])
            if offset == (0, 0):
                part = part + dyg[m, j].astype(F32)

            @pl.when(s > 0)
            def _(j=j, part=part):
                snd[m, j] = part.astype(BF16)
                send_sc(m, j).start()

            @pl.when(s == 0)
            def _(j=j, part=part):
                fp[j] = part.reshape(NODES, OWN, CB)

        @pl.when(s == 0)
        def _():
            def folded(i):
                return [
                    jnp.concatenate([fp[c, i], fp[c + NODES // 2, i]], axis=0).astype(BF16)
                    for c in range(NODES // 2)
                ]

            for q in range(NODES - 1):
                for c, value in enumerate(folded(near(n, OFFSETS[q]))):
                    fs[m, q, :, c * CB : (c + 1) * CB] = value
                send_f(m, q).start()
            for c, value in enumerate(folded(n)):
                fr[m, n, :, c * CB : (c + 1) * CB] = value

        scale = coef_v[m * ROWS : (m + 1) * ROWS, :]
        for k in range(DP):
            for h in range(2):
                value = (dyg[m, 2 * peer(k) + h].astype(F32) * scale).astype(BF16)
                if k == 0:
                    dys[m, h, own_rows, :] = value
                else:
                    dys_send[m, k - 1, h] = value
        for k in range(1, DP):
            send_dy(m, k).start()

    def send_ret():
        return remote(ret, gi, ss_ret.at[0], rs_ret.at[0], section=above)

    @pl.when(s < SECTIONS - 1)
    def _():
        window = pl.ds(pl.multiple_of(lax.div(n, 2) * 16, 16), 16)
        odd = lax.rem(n, 2) == 1
        for j in range(NODES):
            picked = []
            for m in range(MICRO):
                value = dyg[m, j, window, :].astype(F32)
                picked.append(jnp.where(odd, value[OWN:], value[:OWN]))
            ret[:, j * CB : (j + 1) * CB] = jnp.concatenate(picked, axis=0).astype(BF16)
        send_ret().start()

    @pl.when(s >= 2)
    def _():
        exchange()
        gather_inputs()
        prepare()

    def out_copy(which, i):
        staged, array = ((out_g, g_gate), (out_u, g_up), (out_d, g_down))[which]
        rows = pl.ds(i * 256, 256)
        return pltpu.make_async_copy(staged.at[rows, :], array.at[rows, :], s_out.at[which, i])

    for m in range(MICRO):
        for k in range(1, DP):
            j = peer(k)
            rows = pl.ds(pl.multiple_of(j * ROWS, ROWS), ROWS)
            remote(
                dys_send.at[m, 0], dys.at[m, :, rows, :], ss_dy.at[m, k], rs_dy.at[m, j], dp=j
            ).wait_recv()
        for i in range(HID // 256):
            rows = slice(i * 256, (i + 1) * 256)
            for h in range(2):
                cols = slice(h * CB, (h + 1) * CB)
                value = dot(hid_t[m, rows, :], dys[m, h])
                if m == 0:
                    acc_d[rows, cols] = value
                else:
                    out_d[rows, cols] = (acc_d[rows, cols] + value).astype(BF16)
            if m == 1:
                out_copy(2, i).start()
        for k in range(1, DP):
            j = peer(k)
            rows = pl.ds(pl.multiple_of(j * ROWS, ROWS), ROWS)
            remote(
                backs.at[m, own_rows, :], backs.at[m, rows, :], ss_b.at[m, k], rs_b.at[m, j], dp=j
            ).wait_recv()
        for k in range(DP):
            rows = slice(k * ROWS, (k + 1) * ROWS)
            back = backs[m, rows, :].astype(F32)
            gate = gates[m, rows, :].astype(F32)
            sigma = jax.nn.sigmoid(gate)
            dga[rows, :] = (
                back * ups[m, rows, :].astype(F32) * sigma * (1.0 + gate * (1.0 - sigma))
            ).astype(BF16)
            dua[rows, :] = (back * gate * sigma).astype(BF16)
        for which, (d, acc, out) in enumerate(((dga, acc_g, out_g), (dua, acc_u, out_u))):
            for i in range(DB // 256):
                rows = slice(i * 256, (i + 1) * 256)
                value = dot(lin_t[m, rows, :], d[...])
                if m == 0:
                    acc[rows, :] = value
                else:
                    out[rows, :] = (acc[rows, :] + value).astype(BF16)
                    out_copy(which, i).start()

    @pl.when(s == 0)
    def _():
        totals = []
        for m in range(MICRO):
            for offset in OFFSETS:
                j = near(n, offset)
                remote(fs.at[m, 0], fr.at[m, j], ss_f.at[m, 0], rs_f.at[m, j], node=j).wait_recv()
            total = jnp.zeros((16, WIDTH // 2), F32)
            for j in range(NODES):
                total = total + fr[m, j].astype(F32)
            totals.append(total)
        for c in range(2):
            gi[:, c * (WIDTH // 2) : (c + 1) * (WIDTH // 2)] = jnp.concatenate(
                [total[c * OWN : (c + 1) * OWN] for total in totals], axis=0
            ).astype(BF16)

    @pl.when(s > 0)
    def _():
        remote(ret, gi, ss_ret.at[0], rs_ret.at[0], section=below).wait_recv()

    last = pltpu.make_async_copy(gi, grad_in, s_small.at[6])
    last.start()

    @pl.when(s == SECTIONS - 1)
    def _():
        for q in range(NODES - 1):
            send_go(q).wait_send()

    for k in range(1, DP):
        send_gate(k).wait_send()
        send_up(k).wait_send()
        send_lx(k).wait_send()
    for q in range(NODES - 1):
        send_lg(q).wait_send()
    for m in range(MICRO):
        for k in range(1, DP):
            send_b(m, k).wait_send()
            send_dy(m, k).wait_send()

    @pl.when(s < SECTIONS - 1)
    def _():
        for m in range(MICRO):
            for q in range(NODES - 1):
                send_ga(m, q).wait_send()
        send_ret().wait_send()

    @pl.when(s > 0)
    def _():
        for m in range(MICRO):
            for j in range(NODES):
                send_sc(m, j).wait_send()

    @pl.when(s == 0)
    def _():
        for m in range(MICRO):
            for q in range(NODES - 1):
                send_f(m, q).wait_send()

    for which, count in ((0, DB // 256), (1, DB // 256), (2, HID // 256)):
        for i in range(count):
            out_copy(which, i).wait()
    last.wait()


def shards(grad_out, layer_in, gate_pre, up_pre, expert_ids, route_weight, w_gate, w_up, w_down):
    both = MICRO * OWN
    dma = pltpu.SemaphoreType.DMA
    vmem = pltpu.VMEM
    scratch = [
        vmem((WD_SLOTS, HID, CB), BF16),
        vmem((WG_SLOTS, CB, HID), BF16),
        vmem((NODES, CB, HID), BF16),
        vmem((NODES, 2 * HID, CB), BF16),
        vmem((MICRO, 2, ROWS), jnp.int32),
        vmem((MICRO, 2, ROWS), F32),
        vmem((both, WIDTH), BF16),
        vmem((MICRO * ROWS, 1), F32),
        vmem((NODES, both, WIDTH), BF16),
        vmem((MICRO, NODES, ROWS, CB), BF16),
        vmem((MICRO, NODES, ROWS, CB), BF16),
        vmem((MICRO, NODES, ROWS, CB), BF16),
        vmem((MICRO, ROWS, 2 * HID), BF16),
        vmem((MICRO, ALL, HID), BF16),
        vmem((MICRO, ALL, HID), BF16),
        vmem((MICRO, ALL, HID), BF16),
        vmem((MICRO, 2, ALL, CB), BF16),
        vmem((MICRO, DP - 1, 2, ROWS, CB), BF16),
        vmem((DP, both, DB), BF16),
        vmem((DP, both, DB), BF16),
        vmem((NODES, DP, both, DB), BF16),
        vmem((MICRO, DB, ALL), BF16),
        vmem((MICRO, HID, ALL), BF16),
        vmem((ALL, HID), BF16),
        vmem((ALL, HID), BF16),
        vmem((DB, HID), F32),
        vmem((DB, HID), F32),
        vmem((HID, DB), F32),
        vmem((DB, HID), BF16),
        vmem((DB, HID), BF16),
        vmem((HID, DB), BF16),
        vmem((both, WIDTH), BF16),
        vmem((both, WIDTH), BF16),
        vmem((NODES, NODES, OWN, CB), F32),
        vmem((MICRO, NODES - 1, 16, WIDTH // 2), BF16),
        vmem((MICRO, NODES, 16, WIDTH // 2), BF16),
        dma((7,)),
        dma((NODES,)),
        dma((2 * NODES,)),
        dma((3, 4)),
        dma((NODES,)),
        dma((NODES,)),
        dma((MICRO, NODES)),
        dma((MICRO, NODES)),
        dma((MICRO, NODES)),
        dma((MICRO, NODES)),
        dma((DP,)),
        dma((DP,)),
        dma((DP,)),
        dma((DP,)),
        dma((DP,)),
        dma((DP,)),
        dma((NODES,)),
        dma((NODES,)),
        dma((MICRO, DP)),
        dma((MICRO, DP)),
        dma((MICRO, DP)),
        dma((MICRO, DP)),
        dma((1,)),
        dma((1,)),
        dma((MICRO, NODES)),
        dma((MICRO, NODES)),
    ]
    anywhere = pl.BlockSpec(memory_space=pl.ANY)
    grad_in, g_gate, g_up, g_down = pl.pallas_call(
        body,
        out_shape=(
            jax.ShapeDtypeStruct((both, WIDTH), BF16),
            jax.ShapeDtypeStruct((DB, HID), BF16),
            jax.ShapeDtypeStruct((DB, HID), BF16),
            jax.ShapeDtypeStruct((HID, DB), BF16),
        ),
        in_specs=[anywhere] * 9,
        out_specs=(anywhere,) * 4,
        scratch_shapes=scratch,
        compiler_params=pltpu.CompilerParams(
            collective_id=0, has_side_effects=True, vmem_limit_bytes=62 * 2**20
        ),
        cost_estimate=pl.CostEstimate(flops=5 * 10**9, bytes_accessed=24 * 10**6, transcendentals=10**6),
        name="relay",
    )(
        grad_out.reshape(both, WIDTH),
        layer_in.reshape(both, WIDTH),
        gate_pre[0],
        up_pre[0],
        expert_ids[0].transpose(0, 2, 1),
        route_weight[0].transpose(0, 2, 1),
        w_gate[0],
        w_up[0],
        w_down[0],
    )
    return grad_in.reshape(1, MICRO, OWN, WIDTH), g_gate[None], g_up[None], g_down[None]


def solution(mesh):
    return jax.shard_map(
        shards,
        mesh=mesh,
        in_specs=(
            P(None, ("dp", "node"), None),
            P("section", None, ("dp", "node"), None),
            P("section", None, "dp", "node"),
            P("section", None, "dp", "node"),
            P("section", None, "dp", None),
            P("section", None, "dp", None),
            P("section", None, "node"),
            P("section", None, "node"),
            P("section", "node", None),
        ),
        out_specs=(
            P("section", None, ("dp", "node"), None),
            P("section", "dp", "node"),
            P("section", "dp", "node"),
            P("section", "node", "dp"),
        ),
        check_vma=False,
    )
```

```python
import jax
import jax.numpy as jnp
from jax import lax
from jax.experimental import pallas as pl
from jax.experimental.pallas import tpu as pltpu
from jax.sharding import PartitionSpec as P

MESH = pl.DeviceIdType.MESH
F32 = jnp.float32
BF16 = jnp.bfloat16
SECTIONS = 4
DP = 4
NODES = 8
MICRO = 2
OWN = 8
ROWS = OWN * NODES
ALL = ROWS * DP
WIDTH = 3072
HID = 1024
CB = WIDTH // NODES
DB = WIDTH // DP
HALF = WIDTH // 2
OFFSETS = ((1, 2), (1, 1), (1, 3), (1, 0), (0, 2), (0, 1), (0, 3))


def near(n, offset):
    high, x = lax.div(n, 4), lax.rem(n, 4)
    return lax.rem(high + offset[0], 2) * 4 + lax.rem(x + offset[1], 4)


def dot(a, b):
    return lax.dot_general(a, b, (((1,), (0,)), ((), ())), preferred_element_type=F32)


def remote(src, dst, send, recv, **device):
    return pltpu.make_async_remote_copy(
        src_ref=src,
        dst_ref=dst,
        send_sem=send,
        recv_sem=recv,
        device_id=device,
        device_id_type=MESH,
    )


def body(
    grad_out, layer_in, gate_pre, up_pre, ids, route, w_gate, w_up, w_down,
    grad_in, lin_out, dg_out, du_out, gd_out,
    wd_raw, wg_raw, wdt, wgut,
    ids_v, route_v, lin_v, coef_v, factors,
    go, dyg, prt, snd, dgu,
    gates, ups, backs, dys, dys_send,
    lsc, lx, lg, lin_t, hid_t, dga, dua, gd,
    ret, gi, fp, fs, fr,
    s_small, s_wd, s_wg, s_out,
    ss_go, rs_go, ss_sc, rs_sc, ss_ga, rs_ga,
    ss_gate, rs_gate, ss_up, rs_up, ss_lx, rs_lx, ss_lg, rs_lg,
    ss_b, rs_b, ss_dy, rs_dy, ss_ret, rs_ret, ss_f, rs_f,
):
    s = lax.axis_index("section")
    r = lax.axis_index("dp")
    n = lax.axis_index("node")
    above = lax.rem(s + 1, SECTIONS)
    below = lax.rem(s + SECTIONS - 1, SECTIONS)
    own_rows = pl.ds(pl.multiple_of(r * ROWS, ROWS), ROWS)

    def peer(k):
        return lax.rem(r + k, DP)

    barrier = pltpu.get_barrier_semaphore()
    for offset in OFFSETS:
        pl.semaphore_signal(
            barrier, inc=1, device_id={"node": near(n, offset)}, device_id_type=MESH
        )
    for k in range(1, DP):
        pl.semaphore_signal(barrier, inc=1, device_id={"dp": peer(k)}, device_id_type=MESH)

    @pl.when(s < SECTIONS - 1)
    def _():
        for j in range(NODES):
            pl.semaphore_signal(
                barrier, inc=1, device_id={"section": above, "node": j}, device_id_type=MESH
            )

    @pl.when(s > 0)
    def _():
        for j in range(NODES):
            pl.semaphore_signal(
                barrier, inc=1, device_id={"section": below, "node": j}, device_id_type=MESH
            )

    far = lax.rem(s + 2, SECTIONS)

    @pl.when(lax.rem(s, 2) == 1)
    def _():
        for offset in OFFSETS:
            pl.semaphore_signal(
                barrier,
                inc=1,
                device_id={"section": far, "node": near(n, offset)},
                device_id_type=MESH,
            )

    def load_wd(j):
        return pltpu.make_async_copy(w_down.at[:, pl.ds(j * CB, CB)], wd_raw.at[j], s_wd.at[j])

    def load_wg(j):
        ref = w_gate if j % 2 == 0 else w_up
        return pltpu.make_async_copy(
            ref.at[pl.ds((j // 2) * CB, CB), :], wg_raw.at[j], s_wg.at[j]
        )

    small = [
        pltpu.make_async_copy(ids, ids_v, s_small.at[0]),
        pltpu.make_async_copy(route, route_v, s_small.at[1]),
        pltpu.make_async_copy(layer_in, lin_v, s_small.at[2]),
        pltpu.make_async_copy(gate_pre, gates.at[:, own_rows, :], s_small.at[3]),
        pltpu.make_async_copy(up_pre, ups.at[:, own_rows, :], s_small.at[4]),
        pltpu.make_async_copy(grad_out, go.at[n], s_small.at[5]),
    ]
    for copy in small:
        copy.start()
    for j in range(NODES):
        load_wd(j).start()
    for j in range(2 * NODES):
        load_wg(j).start()

    neighbours = jnp.minimum(s, 1) + jnp.minimum(SECTIONS - 1 - s, 1)
    pl.semaphore_wait(
        barrier,
        NODES - 1 + DP - 1 + neighbours * NODES + lax.rem(s, 2) * (NODES - 1),
    )

    def send_go(q, half):
        columns = pl.ds(half * HALF, HALF)
        return remote(
            grad_out.at[:, columns], go.at[n, :, columns], ss_go.at[q], rs_go.at[n, half],
            section=SECTIONS - 1, node=near(n, OFFSETS[q]),
        )

    def send_gate(k):
        return remote(
            gate_pre, gates.at[:, own_rows, :], ss_gate.at[k], rs_gate.at[r], dp=peer(k)
        )

    def send_up(k):
        return remote(
            up_pre, ups.at[:, own_rows, :], ss_up.at[k], rs_up.at[r], dp=peer(k)
        )

    def send_lx(k):
        return remote(
            lsc.at[peer(k)], lx.at[r], ss_lx.at[k], rs_lx.at[r], dp=peer(k)
        )

    def send_lg(q):
        return remote(lx, lg.at[n], ss_lg.at[q], rs_lg.at[n], node=near(n, OFFSETS[q]))

    @pl.when(s == SECTIONS - 1)
    def _():
        for q in range(NODES - 1):
            send_go(q, 0).start()

    @pl.when(s == 1)
    def _():
        for q in range(NODES - 1):
            send_go(q, 1).start()

    for copy in small:
        copy.wait()
    diagonal = lax.broadcasted_iota(jnp.int32, (ROWS, ROWS), 0) == lax.broadcasted_iota(
        jnp.int32, (ROWS, ROWS), 1
    )
    for m in range(MICRO):
        across = jnp.sum(
            jnp.where(ids_v[m] == 0, route_v[m], jnp.float32(0.0)), axis=0, keepdims=True
        )
        coef_v[m * ROWS : (m + 1) * ROWS, :] = jnp.sum(
            jnp.where(diagonal, across, jnp.float32(0.0)), axis=1, keepdims=True
        )

    for m in range(MICRO):
        gate = gates[m, own_rows, :].astype(F32)
        active = jax.nn.sigmoid(gate) * coef_v[m * ROWS : (m + 1) * ROWS, :]
        factors[m, :, :HID] = (
            ups[m, own_rows, :].astype(F32) * active * (1.0 + gate * (1.0 - jax.nn.sigmoid(gate)))
        )
        factors[m, :, HID:] = gate * active

    def exchange():
        scale = jnp.concatenate(
            [
                coef_v[pl.ds(pl.multiple_of(m * ROWS + n * OWN, OWN), OWN), :]
                for m in range(MICRO)
            ],
            axis=0,
        )
        for j in range(DP):
            lsc[j] = (lin_v[:, j * DB : (j + 1) * DB].astype(F32) * scale).astype(BF16)
        lx[r] = lsc[r]
        for k in range(1, DP):
            send_lx(k).start()
        for k in range(1, DP):
            send_gate(k).start()
        for k in range(1, DP):
            send_up(k).start()

    def gather_inputs():
        for k in range(1, DP):
            remote(lsc.at[0], lx.at[peer(k)], ss_lx.at[k], rs_lx.at[peer(k)], dp=peer(k)).wait_recv()
        for q in range(NODES - 1):
            send_lg(q).start()
        lg[n] = lx[...]

    def keep_lin():
        return pltpu.make_async_copy(lin_t, lin_out, s_out.at[0])

    def prepare():
        for offset in OFFSETS:
            j = near(n, offset)
            remote(lx, lg.at[j], ss_lg.at[0], rs_lg.at[j], node=j).wait_recv()
        for m in range(MICRO):
            rows = jnp.concatenate(
                [
                    lg[i, k, :, :].astype(F32)[m * OWN : (m + 1) * OWN]
                    for k in range(DP)
                    for i in range(NODES)
                ],
                axis=0,
            )
            lin_t[:, m * ALL : (m + 1) * ALL] = rows.astype(BF16).T
        keep_lin().start()
        for k in range(1, DP):
            j = peer(k)
            rows = pl.ds(pl.multiple_of(j * ROWS, ROWS), ROWS)
            remote(gate_pre, gates.at[:, rows, :], ss_gate.at[k], rs_gate.at[j], dp=j).wait_recv()
            remote(up_pre, ups.at[:, rows, :], ss_up.at[k], rs_up.at[j], dp=j).wait_recv()
        for m in range(MICRO):
            for c in range(2):
                rows = pl.ds(c * 128, 128)
                g = gates[m, rows, :].astype(F32)
                hidden = (g * jax.nn.sigmoid(g) * ups[m, rows, :].astype(F32)).astype(BF16)
                hid_t[:, m * ALL + c * 128 : m * ALL + (c + 1) * 128] = hidden.T

    @pl.when(s < 2)
    def _():
        exchange()

    for j in range(NODES):
        load_wd(j).wait()
        wdt[j] = wd_raw[j].T
    for j in range(NODES):
        load_wg(2 * j).wait()
        load_wg(2 * j + 1).wait()
        wgut[j, :HID, :] = wg_raw[2 * j].T
        wgut[j, HID:, :] = wg_raw[2 * j + 1].T

    @pl.when(s < 2)
    def _():
        gather_inputs()
        prepare()

    def send_ga(m, q):
        return remote(
            dyg.at[m, n], dyg.at[m, n], ss_ga.at[m, q], rs_ga.at[m, n], node=near(n, OFFSETS[q])
        )

    def recv_ga(m, j):
        return remote(dyg.at[m, j], dyg.at[m, j], ss_ga.at[m, 0], rs_ga.at[m, j], node=j)

    def finish_back(m, back):
        backs[m, own_rows, :] = back.astype(BF16)
        dgu[m, :, :HID] = (back * factors[m, :, :HID]).astype(BF16)
        dgu[m, :, HID:] = (back * factors[m, :, HID:]).astype(BF16)

    def unpack(m, columns):
        block = go[:, :, columns].astype(F32)
        return block[:, m * OWN : (m + 1) * OWN, :].reshape(ROWS, CB).astype(BF16)

    @pl.when(s == SECTIONS - 1)
    def _():
        for half in range(2):
            columns = pl.ds(half * HALF, HALF)
            for offset in OFFSETS:
                j = near(n, offset)
                remote(
                    grad_out.at[:, columns], go.at[j, :, columns], ss_go.at[0], rs_go.at[j, half],
                    section=SECTIONS - 1, node=j,
                ).wait_recv()
        back = jnp.zeros((MICRO * ROWS, HID), F32)
        for j in range(NODES):
            block = go[:, :, j * CB : (j + 1) * CB].reshape(MICRO * ROWS, CB)
            back = back + dot(block, wdt[j])
        back = back.reshape(NODES, MICRO * OWN, HID)
        for m in range(MICRO):
            finish_back(m, back[:, m * OWN : (m + 1) * OWN, :].reshape(ROWS, HID))
            dyg[m, n] = unpack(m, pl.ds(pl.multiple_of(n * CB, CB), CB))

    @pl.when(s < SECTIONS - 1)
    def _():
        for m in range(MICRO):
            for j in range(NODES):
                remote(
                    snd.at[m, j], prt.at[m, j], ss_sc.at[m, j], rs_sc.at[m, j],
                    section=above, node=j,
                ).wait_recv()
            total = prt[m, 0].astype(F32)
            for j in range(1, NODES):
                total = total + prt[m, j].astype(F32)
            dyg[m, n] = total.astype(BF16)
            for q in range(NODES - 1):
                send_ga(m, q).start()

    def send_sc(m, j):
        return remote(
            snd.at[m, j], prt.at[m, n], ss_sc.at[m, j], rs_sc.at[m, n], section=below, node=j
        )

    def send_b(m, k):
        return remote(
            backs.at[m, own_rows, :], backs.at[m, own_rows, :],
            ss_b.at[m, k], rs_b.at[m, r], dp=peer(k),
        )

    def send_dy(m, k):
        return remote(
            dys_send.at[m, k - 1], dys.at[m, :, own_rows, :],
            ss_dy.at[m, k], rs_dy.at[m, r], dp=peer(k),
        )

    def send_f(m, q, step):
        half = (1 - lax.div(n, 4)) if step == 0 else lax.div(n, 4)
        return remote(
            fs.at[m, q, step], fr.at[m, n, half], ss_f.at[m, q, step], rs_f.at[m, n, half],
            node=near(n, OFFSETS[q]),
        )

    def send_tokens(m, step):
        half = (1 - lax.div(n, 4)) if step == 0 else lax.div(n, 4)

        def put(place, i):
            for c in range(2):
                place[:, c * CB : (c + 1) * CB] = jnp.concatenate(
                    [fp[half * 4 + c, i], fp[half * 4 + 2 + c, i]], axis=0
                ).astype(BF16)

        for q in range(NODES - 1):
            put(fs.at[m, q, step], near(n, OFFSETS[q]))
            send_f(m, q, step).start()
        put(fr.at[m, n, half], n)

    def exchange_dy(m):
        scale = coef_v[m * ROWS : (m + 1) * ROWS, :]
        for k in range(DP):
            for h in range(2):
                value = (dyg[m, 2 * peer(k) + h].astype(F32) * scale).astype(BF16)
                if k == 0:
                    dys[m, h, own_rows, :] = value
                else:
                    dys_send[m, k - 1, h] = value
        for k in range(1, DP):
            send_dy(m, k).start()

    arrivals = (((0, 1), (0, 3)), ((0, 2), (1, 0)), ((1, 1), (1, 3), (1, 2)))
    order = OFFSETS + ((0, 0),)
    for m in range(MICRO):

        @pl.when(s < SECTIONS - 1)
        def _():
            back = dot(dyg[m, n], wdt[n])
            for group in arrivals:
                for offset in group:
                    recv_ga(m, near(n, offset)).wait_recv()
                for offset in group:
                    j = near(n, offset)
                    back = back + dot(dyg[m, j], wdt[j])
            finish_back(m, back)

        @pl.when(s == 0)
        def _():
            for k in range(1, DP):
                send_b(m, k).start()
            exchange_dy(m)

        for g in range(NODES // 2):
            for offset in order[2 * g : 2 * g + 2]:
                j = near(n, offset)
                part = dot(dgu[m], wgut[j])
                if offset == (0, 0):
                    part = part + dyg[m, n].astype(F32)
                snd[m, j] = part.astype(BF16)
                fp[j] = part.reshape(NODES, OWN, CB)

            @pl.when(s > 0)
            def _():
                for offset in order[2 * g : 2 * g + 2]:
                    send_sc(m, near(n, offset)).start()

            if g % 2 == 1:

                @pl.when(s == 0)
                def _():
                    send_tokens(m, g // 2)

    @pl.when(s == SECTIONS - 1)
    def _():
        for m in range(MICRO):
            for j in range(NODES):
                dyg[m, j] = unpack(m, slice(j * CB, (j + 1) * CB))

    @pl.when(s > 0)
    def _():
        for m in range(MICRO):
            for k in range(1, DP):
                send_b(m, k).start()
        for m in range(MICRO):
            exchange_dy(m)

    def send_ret():
        return remote(ret, gi, ss_ret.at[0], rs_ret.at[0], section=above)

    @pl.when(s < SECTIONS - 1)
    def _():
        window = pl.ds(pl.multiple_of(lax.div(n, 2) * 16, 16), 16)
        odd = lax.rem(n, 2) == 1
        for j in range(NODES):
            picked = []
            for m in range(MICRO):
                value = dyg[m, j, window, :].astype(F32)
                picked.append(jnp.where(odd, value[OWN:], value[:OWN]))
            ret[:, j * CB : (j + 1) * CB] = jnp.concatenate(picked, axis=0).astype(BF16)
        send_ret().start()

    @pl.when(s >= 2)
    def _():
        exchange()
        gather_inputs()
        prepare()

    def keep_d(which, m):
        staged, array = ((dga, dg_out), (dua, du_out))[which]
        return pltpu.make_async_copy(staged.at[m], array.at[m], s_out.at[1 + 2 * which + m])

    def keep_down(i):
        rows = pl.ds(i * 256, 256)
        return pltpu.make_async_copy(gd.at[rows, :], gd_out.at[rows, :], s_out.at[5 + i])

    def spread(m):
        for k in range(1, DP):
            j = peer(k)
            rows = pl.ds(pl.multiple_of(j * ROWS, ROWS), ROWS)
            remote(
                backs.at[m, own_rows, :], backs.at[m, rows, :], ss_b.at[m, k], rs_b.at[m, j], dp=j
            ).wait_recv()
        for k in range(DP):
            rows = slice(k * ROWS, (k + 1) * ROWS)
            back = backs[m, rows, :].astype(F32)
            gate = gates[m, rows, :].astype(F32)
            sigma = jax.nn.sigmoid(gate)
            dga[m, rows, :] = (
                back * ups[m, rows, :].astype(F32) * sigma * (1.0 + gate * (1.0 - sigma))
            ).astype(BF16)
            dua[m, rows, :] = (back * gate * sigma).astype(BF16)
        keep_d(0, m).start()
        keep_d(1, m).start()

    spread(0)
    for m in range(MICRO):
        for k in range(1, DP):
            j = peer(k)
            rows = pl.ds(pl.multiple_of(j * ROWS, ROWS), ROWS)
            remote(
                dys_send.at[m, 0], dys.at[m, :, rows, :], ss_dy.at[m, k], rs_dy.at[m, j], dp=j
            ).wait_recv()
    for i in range(HID // 256):
        rows = slice(i * 256, (i + 1) * 256)
        for h in range(2):
            value = dot(hid_t[rows, :ALL], dys[0, h]) + dot(hid_t[rows, ALL:], dys[1, h])
            gd[rows, h * CB : (h + 1) * CB] = value.astype(BF16)
        keep_down(i).start()
    spread(1)

    @pl.when(s == 0)
    def _():
        for m in range(MICRO):
            for offset in OFFSETS:
                j = near(n, offset)
                for half in range(2):
                    remote(
                        fs.at[m, 0, half], fr.at[m, j, half], ss_f.at[m, 0, half],
                        rs_f.at[m, j, half], node=j,
                    ).wait_recv()
        for half in range(2):
            totals = []
            for m in range(MICRO):
                total = fr[m, 0, half].astype(F32)
                for j in range(1, NODES):
                    total = total + fr[m, j, half].astype(F32)
                totals.append(total)
            for c in range(2):
                start = half * HALF + c * 2 * CB
                gi[:, start : start + 2 * CB] = jnp.concatenate(
                    [total[c * OWN : (c + 1) * OWN] for total in totals], axis=0
                ).astype(BF16)

    @pl.when(s > 0)
    def _():
        remote(ret, gi, ss_ret.at[0], rs_ret.at[0], section=below).wait_recv()

    last = pltpu.make_async_copy(gi, grad_in, s_small.at[6])
    last.start()

    @pl.when(s == SECTIONS - 1)
    def _():
        for q in range(NODES - 1):
            send_go(q, 0).wait_send()

    @pl.when(s == 1)
    def _():
        for q in range(NODES - 1):
            send_go(q, 1).wait_send()

    for k in range(1, DP):
        send_gate(k).wait_send()
        send_up(k).wait_send()
        send_lx(k).wait_send()
    for q in range(NODES - 1):
        send_lg(q).wait_send()
    for m in range(MICRO):
        for k in range(1, DP):
            send_b(m, k).wait_send()
            send_dy(m, k).wait_send()

    @pl.when(s < SECTIONS - 1)
    def _():
        for m in range(MICRO):
            for q in range(NODES - 1):
                send_ga(m, q).wait_send()
        send_ret().wait_send()

    @pl.when(s > 0)
    def _():
        for m in range(MICRO):
            for j in range(NODES):
                send_sc(m, j).wait_send()

    @pl.when(s == 0)
    def _():
        for m in range(MICRO):
            for q in range(NODES - 1):
                for step in range(2):
                    send_f(m, q, step).wait_send()

    keep_lin().wait()
    for m in range(MICRO):
        keep_d(0, m).wait()
        keep_d(1, m).wait()
    for i in range(HID // 256):
        keep_down(i).wait()
    last.wait()


def finish(
    grad_in, lin, dg, du, down,
    o_in, o_gate, o_up, o_down,
    in_v, lin_v, dg_v, du_v, down_v, gate_v, up_v, sems,
):
    loads = [
        pltpu.make_async_copy(lin, lin_v, sems.at[0]),
        pltpu.make_async_copy(dg, dg_v, sems.at[1]),
        pltpu.make_async_copy(du, du_v, sems.at[2]),
        pltpu.make_async_copy(down, down_v, sems.at[3]),
        pltpu.make_async_copy(grad_in, in_v, sems.at[4]),
    ]
    for copy in loads:
        copy.start()
    stores = []
    loads[0].wait()
    for which, (d, staged, out) in enumerate(((dg_v, gate_v, o_gate), (du_v, up_v, o_up))):
        loads[1 + which].wait()
        for i in range(DB // 256):
            rows = pl.ds(i * 256, 256)
            value = dot(lin_v[rows, :ALL], d[0]) + dot(lin_v[rows, ALL:], d[1])
            staged[rows, :] = value.astype(BF16)
            stores.append(
                pltpu.make_async_copy(
                    staged.at[rows, :], out.at[rows, :], sems.at[7 + 3 * which + i]
                )
            )
            stores[-1].start()
        if which == 0:
            loads[3].wait()
            loads[4].wait()
            stores.append(pltpu.make_async_copy(down_v, o_down, sems.at[5]))
            stores.append(pltpu.make_async_copy(in_v, o_in, sems.at[6]))
            stores[-2].start()
            stores[-1].start()
    for copy in stores:
        copy.wait()


def shards(grad_out, layer_in, gate_pre, up_pre, expert_ids, route_weight, w_gate, w_up, w_down):
    both = MICRO * OWN
    dma = pltpu.SemaphoreType.DMA
    vmem = pltpu.VMEM
    scratch = [
        vmem((NODES, HID, CB), BF16),
        vmem((2 * NODES, CB, HID), BF16),
        vmem((NODES, CB, HID), BF16),
        vmem((NODES, 2 * HID, CB), BF16),
        vmem((MICRO, 2, ROWS), jnp.int32),
        vmem((MICRO, 2, ROWS), F32),
        vmem((both, WIDTH), BF16),
        vmem((MICRO * ROWS, 1), F32),
        vmem((MICRO, ROWS, 2 * HID), F32),
        vmem((NODES, both, WIDTH), BF16),
        vmem((MICRO, NODES, ROWS, CB), BF16),
        vmem((MICRO, NODES, ROWS, CB), BF16),
        vmem((MICRO, NODES, ROWS, CB), BF16),
        vmem((MICRO, ROWS, 2 * HID), BF16),
        vmem((MICRO, ALL, HID), BF16),
        vmem((MICRO, ALL, HID), BF16),
        vmem((MICRO, ALL, HID), BF16),
        vmem((MICRO, 2, ALL, CB), BF16),
        vmem((MICRO, DP - 1, 2, ROWS, CB), BF16),
        vmem((DP, both, DB), BF16),
        vmem((DP, both, DB), BF16),
        vmem((NODES, DP, both, DB), BF16),
        vmem((DB, MICRO * ALL), BF16),
        vmem((HID, MICRO * ALL), BF16),
        vmem((MICRO, ALL, HID), BF16),
        vmem((MICRO, ALL, HID), BF16),
        vmem((HID, DB), BF16),
        vmem((both, WIDTH), BF16),
        vmem((both, WIDTH), BF16),
        vmem((NODES, NODES, OWN, CB), F32),
        vmem((MICRO, NODES - 1, 2, 16, 2 * CB), BF16),
        vmem((MICRO, NODES, 2, 16, 2 * CB), BF16),
        dma((7,)),
        dma((NODES,)),
        dma((2 * NODES,)),
        dma((9,)),
        dma((NODES,)),
        dma((NODES, 2)),
        dma((MICRO, NODES)),
        dma((MICRO, NODES)),
        dma((MICRO, NODES)),
        dma((MICRO, NODES)),
        dma((DP,)),
        dma((DP,)),
        dma((DP,)),
        dma((DP,)),
        dma((DP,)),
        dma((DP,)),
        dma((NODES,)),
        dma((NODES,)),
        dma((MICRO, DP)),
        dma((MICRO, DP)),
        dma((MICRO, DP)),
        dma((MICRO, DP)),
        dma((1,)),
        dma((1,)),
        dma((MICRO, NODES, 2)),
        dma((MICRO, NODES, 2)),
    ]
    anywhere = pl.BlockSpec(memory_space=pl.ANY)
    left = pl.pallas_call(
        body,
        out_shape=(
            jax.ShapeDtypeStruct((both, WIDTH), BF16),
            jax.ShapeDtypeStruct((DB, MICRO * ALL), BF16),
            jax.ShapeDtypeStruct((MICRO, ALL, HID), BF16),
            jax.ShapeDtypeStruct((MICRO, ALL, HID), BF16),
            jax.ShapeDtypeStruct((HID, DB), BF16),
        ),
        in_specs=[anywhere] * 9,
        out_specs=(anywhere,) * 5,
        scratch_shapes=scratch,
        compiler_params=pltpu.CompilerParams(
            collective_id=0, has_side_effects=True, vmem_limit_bytes=62 * 2**20
        ),
        cost_estimate=pl.CostEstimate(flops=5 * 10**9, bytes_accessed=24 * 10**6, transcendentals=10**6),
        name="relay",
    )(
        grad_out.reshape(both, WIDTH),
        layer_in.reshape(both, WIDTH),
        gate_pre[0],
        up_pre[0],
        expert_ids[0].transpose(0, 2, 1),
        route_weight[0].transpose(0, 2, 1),
        w_gate[0],
        w_up[0],
        w_down[0],
    )
    grad_in, g_gate, g_up, g_down = pl.pallas_call(
        finish,
        out_shape=(
            jax.ShapeDtypeStruct((both, WIDTH), BF16),
            jax.ShapeDtypeStruct((DB, HID), BF16),
            jax.ShapeDtypeStruct((DB, HID), BF16),
            jax.ShapeDtypeStruct((HID, DB), BF16),
        ),
        in_specs=[anywhere] * 5,
        out_specs=(anywhere,) * 4,
        scratch_shapes=[
            vmem((both, WIDTH), BF16),
            vmem((DB, MICRO * ALL), BF16),
            vmem((MICRO, ALL, HID), BF16),
            vmem((MICRO, ALL, HID), BF16),
            vmem((HID, DB), BF16),
            vmem((DB, HID), BF16),
            vmem((DB, HID), BF16),
            dma((13,)),
        ],
        compiler_params=pltpu.CompilerParams(vmem_limit_bytes=62 * 2**20),
        cost_estimate=pl.CostEstimate(flops=16 * 10**8, bytes_accessed=10**7, transcendentals=0),
        name="finish",
    )(*left)
    return grad_in.reshape(1, MICRO, OWN, WIDTH), g_gate[None], g_up[None], g_down[None]


def solution(mesh):
    return jax.shard_map(
        shards,
        mesh=mesh,
        in_specs=(
            P(None, ("dp", "node"), None),
            P("section", None, ("dp", "node"), None),
            P("section", None, "dp", "node"),
            P("section", None, "dp", "node"),
            P("section", None, "dp", None),
            P("section", None, "dp", None),
            P("section", None, "node"),
            P("section", None, "node"),
            P("section", "node", None),
        ),
        out_specs=(
            P("section", None, ("dp", "node"), None),
            P("section", "dp", "node"),
            P("section", "dp", "node"),
            P("section", "node", "dp"),
        ),
        check_vma=False,
    )
```

```python
import jax
import jax.numpy as jnp
from jax import lax
from jax.experimental import pallas as pl
from jax.experimental.pallas import tpu as pltpu
from jax.sharding import PartitionSpec as P

MESH = pl.DeviceIdType.MESH
F32 = jnp.float32
BF16 = jnp.bfloat16
SECTIONS = 4
DP = 4
NODES = 8
MICRO = 2
OWN = 8
ROWS = OWN * NODES
ALL = ROWS * DP
WIDTH = 3072
HID = 1024
CB = WIDTH // NODES
DB = WIDTH // DP
HALF = WIDTH // 2
WINDOW = 10
PIECES = 3 * NODES
OFFSETS = ((1, 2), (1, 1), (1, 3), (1, 0), (0, 2), (0, 1), (0, 3))


def near(n, offset):
    high, x = lax.div(n, 4), lax.rem(n, 4)
    return lax.rem(high + offset[0], 2) * 4 + lax.rem(x + offset[1], 4)


def dot(a, b):
    return lax.dot_general(a, b, (((1,), (0,)), ((), ())), preferred_element_type=F32)


def remote(src, dst, send, recv, **device):
    return pltpu.make_async_remote_copy(
        src_ref=src,
        dst_ref=dst,
        send_sem=send,
        recv_sem=recv,
        device_id=device,
        device_id_type=MESH,
    )


def body(
    grad_out, layer_in, gate_pre, up_pre, ids, route, w_gate, w_up, w_down,
    grad_in, lin_out, dg_out, du_out, gd_out,
    wd_raw, wg_raw, wdt, wgut,
    ids_v, route_v, lin_v, coef_v, factors,
    go, dyg, prt, snd, dgu,
    gates, ups, backs, dys, crow,
    lsc, lx, lg, lin_t, hid_t, dga, dua, gd,
    ret, gi, fp, fs, fr,
    s_small, s_wd, s_wg, s_out,
    ss_go, rs_go, ss_sc, rs_sc, ss_ga, rs_ga,
    ss_gate, rs_gate, ss_up, rs_up, ss_lx, rs_lx, ss_lg, rs_lg,
    ss_cr, rs_cr, ss_b, rs_b, ss_dy, rs_dy, ss_ret, rs_ret, ss_f, rs_f,
):
    s = lax.axis_index("section")
    r = lax.axis_index("dp")
    n = lax.axis_index("node")
    above = lax.rem(s + 1, SECTIONS)
    below = lax.rem(s + SECTIONS - 1, SECTIONS)

    def peer(k):
        return lax.rem(r + k, DP)

    def load(i):
        if i < NODES:
            return pltpu.make_async_copy(
                w_down.at[pl.ds(i * (HID // NODES), HID // NODES), :], wd_raw.at[i], s_wd.at[i]
            )
        j = i - NODES
        ref = w_gate if j % 2 == 0 else w_up
        return pltpu.make_async_copy(
            ref.at[pl.ds((j // 2) * CB, CB), :], wg_raw.at[j], s_wg.at[j]
        )

    def turn(i):
        load(i).wait()
        if i + WINDOW < PIECES:
            load(i + WINDOW).start()
        if i < NODES:
            rows = slice(i * (HID // NODES), (i + 1) * (HID // NODES))
            for j in range(NODES):
                wdt[j, :, rows] = wd_raw[i, :, j * CB : (j + 1) * CB].T
        else:
            j = i - NODES
            start = (j % 2) * HID
            wgut[j // 2, start : start + HID, :] = wg_raw[j].T

    small = [
        pltpu.make_async_copy(ids, ids_v, s_small.at[0]),
        pltpu.make_async_copy(route, route_v, s_small.at[1]),
        pltpu.make_async_copy(layer_in, lin_v, s_small.at[2]),
        pltpu.make_async_copy(gate_pre, gates.at[r], s_small.at[3]),
        pltpu.make_async_copy(up_pre, ups.at[r], s_small.at[4]),
        pltpu.make_async_copy(grad_out.at[:, :HALF], go.at[n, 0], s_small.at[5]),
        pltpu.make_async_copy(grad_out.at[:, HALF:], go.at[n, 1], s_small.at[6]),
    ]
    for copy in small:
        copy.start()
    for i in range(WINDOW):
        load(i).start()

    barrier = pltpu.get_barrier_semaphore()
    for offset in OFFSETS:
        pl.semaphore_signal(
            barrier, inc=1, device_id={"node": near(n, offset)}, device_id_type=MESH
        )
    for k in range(1, DP):
        pl.semaphore_signal(barrier, inc=1, device_id={"dp": peer(k)}, device_id_type=MESH)

    @pl.when(s < SECTIONS - 1)
    def _():
        for j in range(NODES):
            pl.semaphore_signal(
                barrier, inc=1, device_id={"section": above, "node": j}, device_id_type=MESH
            )

    @pl.when(s > 0)
    def _():
        for j in range(NODES):
            pl.semaphore_signal(
                barrier, inc=1, device_id={"section": below, "node": j}, device_id_type=MESH
            )

    far = lax.rem(s + 2, SECTIONS)

    @pl.when(lax.rem(s, 2) == 1)
    def _():
        for offset in OFFSETS:
            pl.semaphore_signal(
                barrier,
                inc=1,
                device_id={"section": far, "node": near(n, offset)},
                device_id_type=MESH,
            )

    for copy in small:
        copy.wait()
    diagonal = lax.broadcasted_iota(jnp.int32, (ROWS, ROWS), 0) == lax.broadcasted_iota(
        jnp.int32, (ROWS, ROWS), 1
    )
    for m in range(MICRO):
        across = jnp.sum(
            jnp.where(ids_v[m] == 0, route_v[m], jnp.float32(0.0)), axis=0, keepdims=True
        )
        crow[r, 0:1, m * ROWS : (m + 1) * ROWS] = across
        coef_v[m * ROWS : (m + 1) * ROWS, :] = jnp.sum(
            jnp.where(diagonal, across, jnp.float32(0.0)), axis=1, keepdims=True
        )

    for i in range(NODES):
        turn(i)

    neighbours = jnp.minimum(s, 1) + jnp.minimum(SECTIONS - 1 - s, 1)
    pl.semaphore_wait(
        barrier,
        NODES - 1 + DP - 1 + neighbours * NODES + lax.rem(s, 2) * (NODES - 1),
    )

    def send_go(q, half):
        return remote(
            go.at[n, half], go.at[n, half], ss_go.at[q], rs_go.at[n, half],
            section=SECTIONS - 1, node=near(n, OFFSETS[q]),
        )

    def send_gate(k):
        return remote(gates.at[r], gates.at[r], ss_gate.at[k], rs_gate.at[r], dp=peer(k))

    def send_up(k):
        return remote(ups.at[r], ups.at[r], ss_up.at[k], rs_up.at[r], dp=peer(k))

    def send_lx(k):
        return remote(
            lsc.at[peer(k)], lx.at[r], ss_lx.at[k], rs_lx.at[r], dp=peer(k)
        )

    def send_cr(k):
        return remote(crow.at[r], crow.at[r], ss_cr.at[k], rs_cr.at[r], dp=peer(k))

    def send_lg(q):
        return remote(lx, lg.at[n], ss_lg.at[q], rs_lg.at[n], node=near(n, OFFSETS[q]))

    @pl.when(s == SECTIONS - 1)
    def _():
        for q in range(NODES - 1):
            send_go(q, 0).start()

    @pl.when(s == 1)
    def _():
        for q in range(NODES - 1):
            send_go(q, 1).start()

    for m in range(MICRO):
        gate = gates[r, m].astype(F32)
        active = jax.nn.sigmoid(gate) * coef_v[m * ROWS : (m + 1) * ROWS, :]
        factors[m, :, :HID] = (
            ups[r, m].astype(F32) * active * (1.0 + gate * (1.0 - jax.nn.sigmoid(gate)))
        )
        factors[m, :, HID:] = gate * active

    def exchange():
        scale = jnp.concatenate(
            [
                coef_v[pl.ds(pl.multiple_of(m * ROWS + n * OWN, OWN), OWN), :]
                for m in range(MICRO)
            ],
            axis=0,
        )
        for j in range(DP):
            lsc[j] = (lin_v[:, j * DB : (j + 1) * DB].astype(F32) * scale).astype(BF16)
        lx[r] = lsc[r]
        for k in range(1, DP):
            send_cr(k).start()
            send_lx(k).start()
        for k in range(1, DP):
            send_gate(k).start()
        for k in range(1, DP):
            send_up(k).start()

    def take_gates():
        for k in range(1, DP):
            j = peer(k)
            remote(gates.at[r], gates.at[j], ss_gate.at[k], rs_gate.at[j], dp=j).wait_recv()

    def prepare_hidden():
        for k in range(1, DP):
            j = peer(k)
            remote(ups.at[r], ups.at[j], ss_up.at[k], rs_up.at[j], dp=j).wait_recv()
            remote(crow.at[r], crow.at[j], ss_cr.at[k], rs_cr.at[j], dp=j).wait_recv()
        for m in range(MICRO):
            for c in range(2):
                pair = slice(2 * c, 2 * c + 2)
                g = gates[pair, m].reshape(2 * ROWS, HID).astype(F32)
                u = ups[pair, m].reshape(2 * ROWS, HID).astype(F32)
                hidden = (g * jax.nn.sigmoid(g) * u).astype(BF16)
                across = jnp.concatenate(
                    [crow[2 * c + i, 0:1, m * ROWS : (m + 1) * ROWS] for i in range(2)], axis=1
                )
                hid_t[:, m * ALL + c * 128 : m * ALL + (c + 1) * 128] = (
                    hidden.T.astype(F32) * across
                ).astype(BF16)

    def keep_lin():
        return pltpu.make_async_copy(lin_t, lin_out, s_out.at[0])

    def gather_inputs():
        for k in range(1, DP):
            remote(lsc.at[0], lx.at[peer(k)], ss_lx.at[k], rs_lx.at[peer(k)], dp=peer(k)).wait_recv()
        lg[n] = lx[...]
        for q in range(NODES - 1):
            send_lg(q).start()

    def prepare_inputs():
        for offset in OFFSETS:
            j = near(n, offset)
            remote(lx, lg.at[j], ss_lg.at[0], rs_lg.at[j], node=j).wait_recv()
        for m in range(MICRO):
            rows = jnp.concatenate(
                [
                    lg[i, k, :, :].astype(F32)[m * OWN : (m + 1) * OWN]
                    for k in range(DP)
                    for i in range(NODES)
                ],
                axis=0,
            )
            lin_t[:, m * ALL : (m + 1) * ALL] = rows.astype(BF16).T
        keep_lin().start()

    @pl.when(s < 2)
    def _():
        exchange()

    for i in range(NODES, PIECES):
        turn(i)

    @pl.when(s < 2)
    def _():
        gather_inputs()
        take_gates()

    @pl.when(s == 0)
    def _():
        prepare_hidden()
        prepare_inputs()

    def send_ga(m, q):
        return remote(
            dyg.at[m, n], dyg.at[m, n], ss_ga.at[m, q], rs_ga.at[m, n], node=near(n, OFFSETS[q])
        )

    def recv_ga(m, j):
        return remote(dyg.at[m, j], dyg.at[m, j], ss_ga.at[m, 0], rs_ga.at[m, j], node=j)

    def finish_back(m, back):
        backs[m, r] = back.astype(BF16)
        dgu[m, :, :HID] = (back * factors[m, :, :HID]).astype(BF16)
        dgu[m, :, HID:] = (back * factors[m, :, HID:]).astype(BF16)

    def unpack(m, half, columns):
        block = go[:, half, :, columns].astype(F32)
        return block[:, m * OWN : (m + 1) * OWN, :].reshape(ROWS, CB).astype(BF16)

    @pl.when(s == SECTIONS - 1)
    def _():
        for half in range(2):
            for offset in OFFSETS:
                j = near(n, offset)
                remote(
                    go.at[n, half], go.at[j, half], ss_go.at[0], rs_go.at[j, half],
                    section=SECTIONS - 1, node=j,
                ).wait_recv()
        back = jnp.zeros((MICRO * ROWS, HID), F32)
        for j in range(NODES):
            start = (j % 4) * CB
            block = go[:, j // 4, :, start : start + CB].reshape(MICRO * ROWS, CB)
            back = back + dot(block, wdt[j])
        back = back.reshape(NODES, MICRO * OWN, HID)
        for m in range(MICRO):
            finish_back(m, back[:, m * OWN : (m + 1) * OWN, :].reshape(ROWS, HID))
            dyg[m, n] = unpack(m, lax.div(n, 4), pl.ds(pl.multiple_of(lax.rem(n, 4) * CB, CB), CB))

    @pl.when(s < SECTIONS - 1)
    def _():
        for m in range(MICRO):
            for j in range(NODES):
                remote(
                    snd.at[m, j], prt.at[m, j], ss_sc.at[m, j], rs_sc.at[m, j],
                    section=above, node=j,
                ).wait_recv()
            total = prt[m, 0].astype(F32)
            for j in range(1, NODES):
                total = total + prt[m, j].astype(F32)
            dyg[m, n] = total.astype(BF16)
            for q in range(NODES - 1):
                send_ga(m, q).start()

    def send_sc(m, j):
        return remote(
            snd.at[m, j], prt.at[m, n], ss_sc.at[m, j], rs_sc.at[m, n], section=below, node=j
        )

    def send_b(m, k):
        return remote(backs.at[m, r], backs.at[m, r], ss_b.at[m, k], rs_b.at[m, r], dp=peer(k))

    def send_dy(m, k):
        return remote(
            dyg.at[m, pl.ds(2 * peer(k), 2)], dys.at[m, r], ss_dy.at[m, k], rs_dy.at[m, r],
            dp=peer(k),
        )

    def send_f(m, q, step):
        half = (1 - lax.div(n, 4)) if step == 0 else lax.div(n, 4)
        return remote(
            fs.at[m, q, step], fr.at[m, n, half], ss_f.at[m, q, step], rs_f.at[m, n, half],
            node=near(n, OFFSETS[q]),
        )

    def send_tokens(m, step):
        half = (1 - lax.div(n, 4)) if step == 0 else lax.div(n, 4)

        def put(place, i):
            for c in range(2):
                place[:, c * CB : (c + 1) * CB] = jnp.concatenate(
                    [fp[half * 4 + c, i], fp[half * 4 + 2 + c, i]], axis=0
                ).astype(BF16)

        for q in range(NODES - 1):
            put(fs.at[m, q, step], near(n, OFFSETS[q]))
            send_f(m, q, step).start()
        put(fr.at[m, n, half], n)

    def exchange_dy(m):
        for k in range(1, DP):
            send_dy(m, k).start()
        dys[m, r] = dyg[m, pl.ds(2 * r, 2)]

    def exchange_back(m):
        for k in range(1, DP):
            send_b(m, k).start()

    arrivals = (((0, 1), (0, 3)), ((0, 2), (1, 0)), ((1, 1), (1, 3), (1, 2)))
    order = OFFSETS + ((0, 0),)
    for m in range(MICRO):

        @pl.when(s < SECTIONS - 1)
        def _():
            back = dot(dyg[m, n], wdt[n])
            for group in arrivals:
                for offset in group:
                    recv_ga(m, near(n, offset)).wait_recv()
                if group is arrivals[-1]:

                    @pl.when(s == 0)
                    def _():
                        exchange_dy(m)

                for offset in group:
                    j = near(n, offset)
                    back = back + dot(dyg[m, j], wdt[j])
            finish_back(m, back)

        @pl.when(s == 0)
        def _():
            exchange_back(m)

        for g in range(NODES // 2):
            for offset in order[2 * g : 2 * g + 2]:
                j = near(n, offset)
                part = dot(dgu[m], wgut[j])
                if offset == (0, 0):
                    part = part + dyg[m, n].astype(F32)
                snd[m, j] = part.astype(BF16)
                fp[j] = part.reshape(NODES, OWN, CB)

            @pl.when(s > 0)
            def _():
                for offset in order[2 * g : 2 * g + 2]:
                    send_sc(m, near(n, offset)).start()

            if g % 2 == 1:

                @pl.when(s == 0)
                def _():
                    send_tokens(m, g // 2)

        @pl.when(jnp.logical_and(s > 0, s < SECTIONS - 1))
        def _():
            exchange_back(m)
            exchange_dy(m)

    @pl.when(s == SECTIONS - 1)
    def _():
        for m in range(MICRO):
            for j in range(NODES):
                start = (j % 4) * CB
                dyg[m, j] = unpack(m, j // 4, slice(start, start + CB))

        for m in range(MICRO):
            exchange_back(m)
            exchange_dy(m)

    def send_ret():
        return remote(ret, gi, ss_ret.at[0], rs_ret.at[0], section=above)

    @pl.when(s < SECTIONS - 1)
    def _():
        window = pl.ds(pl.multiple_of(lax.div(n, 2) * 16, 16), 16)
        odd = lax.rem(n, 2) == 1
        for j in range(NODES):
            picked = []
            for m in range(MICRO):
                value = dyg[m, j, window, :].astype(F32)
                picked.append(jnp.where(odd, value[OWN:], value[:OWN]))
            ret[:, j * CB : (j + 1) * CB] = jnp.concatenate(picked, axis=0).astype(BF16)
        send_ret().start()

    @pl.when(s >= 2)
    def _():
        exchange()

    @pl.when(s == 2)
    def _():
        gather_inputs()

    @pl.when(s >= 2)
    def _():
        take_gates()

    @pl.when(s > 0)
    def _():
        prepare_hidden()

    def take_ret():
        remote(ret, gi, ss_ret.at[0], rs_ret.at[0], section=below).wait_recv()

    @pl.when(s == SECTIONS - 1)
    def _():
        take_ret()
        gather_inputs()

    @pl.when(s > 0)
    def _():
        prepare_inputs()

    def keep_d(which, m):
        staged, array = ((dga, dg_out), (dua, du_out))[which]
        return pltpu.make_async_copy(staged.at[m], array.at[m], s_out.at[1 + 2 * which + m])

    def keep_down(i):
        rows = pl.ds(i * 256, 256)
        return pltpu.make_async_copy(gd.at[rows, :], gd_out.at[rows, :], s_out.at[5 + i])

    def spread(m):
        for k in range(1, DP):
            j = peer(k)
            remote(backs.at[m, r], backs.at[m, j], ss_b.at[m, k], rs_b.at[m, j], dp=j).wait_recv()
        for k in range(DP):
            rows = slice(k * ROWS, (k + 1) * ROWS)
            back = backs[m, k].astype(F32)
            gate = gates[k, m].astype(F32)
            sigma = jax.nn.sigmoid(gate)
            dga[m, rows, :] = (
                back * ups[k, m].astype(F32) * sigma * (1.0 + gate * (1.0 - sigma))
            ).astype(BF16)
            dua[m, rows, :] = (back * gate * sigma).astype(BF16)
        keep_d(0, m).start()
        keep_d(1, m).start()

    spread(0)
    for m in range(MICRO):
        for k in range(1, DP):
            j = peer(k)
            remote(
                dyg.at[m, pl.ds(0, 2)], dys.at[m, j], ss_dy.at[m, k], rs_dy.at[m, j], dp=j
            ).wait_recv()
    for i in range(HID // 256):
        rows = slice(i * 256, (i + 1) * 256)
        for h in range(2):
            value = dot(hid_t[rows, :ALL], dys[0, :, h].reshape(ALL, CB))
            value = value + dot(hid_t[rows, ALL:], dys[1, :, h].reshape(ALL, CB))
            gd[rows, h * CB : (h + 1) * CB] = value.astype(BF16)
        keep_down(i).start()

    @pl.when(s == 0)
    def _():
        for m in range(MICRO):
            for offset in OFFSETS:
                j = near(n, offset)
                for half in range(2):
                    remote(
                        fs.at[m, 0, half], fr.at[m, j, half], ss_f.at[m, 0, half],
                        rs_f.at[m, j, half], node=j,
                    ).wait_recv()
        for half in range(2):
            totals = []
            for m in range(MICRO):
                total = fr[m, 0, half].astype(F32)
                for j in range(1, NODES):
                    total = total + fr[m, j, half].astype(F32)
                totals.append(total)
            for c in range(2):
                start = half * HALF + c * 2 * CB
                gi[:, start : start + 2 * CB] = jnp.concatenate(
                    [total[c * OWN : (c + 1) * OWN] for total in totals], axis=0
                ).astype(BF16)

    @pl.when(jnp.logical_and(s > 0, s < SECTIONS - 1))
    def _():
        take_ret()

    last = pltpu.make_async_copy(gi, grad_in, s_small.at[7])
    last.start()
    spread(1)

    @pl.when(s == SECTIONS - 1)
    def _():
        for q in range(NODES - 1):
            send_go(q, 0).wait_send()

    @pl.when(s == 1)
    def _():
        for q in range(NODES - 1):
            send_go(q, 1).wait_send()

    for k in range(1, DP):
        send_gate(k).wait_send()
        send_up(k).wait_send()
        send_lx(k).wait_send()
        send_cr(k).wait_send()
    for q in range(NODES - 1):
        send_lg(q).wait_send()
    for m in range(MICRO):
        for k in range(1, DP):
            send_b(m, k).wait_send()
            send_dy(m, k).wait_send()

    @pl.when(s < SECTIONS - 1)
    def _():
        for m in range(MICRO):
            for q in range(NODES - 1):
                send_ga(m, q).wait_send()
        send_ret().wait_send()

    @pl.when(s > 0)
    def _():
        for m in range(MICRO):
            for j in range(NODES):
                send_sc(m, j).wait_send()

    @pl.when(s == 0)
    def _():
        for m in range(MICRO):
            for q in range(NODES - 1):
                for step in range(2):
                    send_f(m, q, step).wait_send()

    keep_lin().wait()
    for m in range(MICRO):
        keep_d(0, m).wait()
        keep_d(1, m).wait()
    for i in range(HID // 256):
        keep_down(i).wait()
    last.wait()


def finish(
    grad_in, lin, dg, du, down,
    o_in, o_gate, o_up, o_down,
    in_v, lin_v, dg_v, du_v, down_v, gate_v, up_v, sems,
):
    loads = [
        pltpu.make_async_copy(lin, lin_v, sems.at[0]),
        pltpu.make_async_copy(dg, dg_v, sems.at[1]),
        pltpu.make_async_copy(du, du_v, sems.at[2]),
        pltpu.make_async_copy(down, down_v, sems.at[3]),
        pltpu.make_async_copy(grad_in, in_v, sems.at[4]),
    ]
    for copy in loads:
        copy.start()
    stores = []
    loads[0].wait()
    for which, (d, staged, out) in enumerate(((dg_v, gate_v, o_gate), (du_v, up_v, o_up))):
        loads[1 + which].wait()
        for i in range(DB // 256):
            rows = pl.ds(i * 256, 256)
            value = dot(lin_v[rows, :ALL], d[0]) + dot(lin_v[rows, ALL:], d[1])
            staged[rows, :] = value.astype(BF16)
            stores.append(
                pltpu.make_async_copy(
                    staged.at[rows, :], out.at[rows, :], sems.at[7 + 3 * which + i]
                )
            )
            stores[-1].start()
        if which == 0:
            loads[3].wait()
            loads[4].wait()
            stores.append(pltpu.make_async_copy(down_v, o_down, sems.at[5]))
            stores.append(pltpu.make_async_copy(in_v, o_in, sems.at[6]))
            stores[-2].start()
            stores[-1].start()
    for copy in stores:
        copy.wait()


def shards(grad_out, layer_in, gate_pre, up_pre, expert_ids, route_weight, w_gate, w_up, w_down):
    both = MICRO * OWN
    dma = pltpu.SemaphoreType.DMA
    vmem = pltpu.VMEM
    scratch = [
        vmem((NODES, HID // NODES, WIDTH), BF16),
        vmem((2 * NODES, CB, HID), BF16),
        vmem((NODES, CB, HID), BF16),
        vmem((NODES, 2 * HID, CB), BF16),
        vmem((MICRO, 2, ROWS), jnp.int32),
        vmem((MICRO, 2, ROWS), F32),
        vmem((both, WIDTH), BF16),
        vmem((MICRO * ROWS, 1), F32),
        vmem((MICRO, ROWS, 2 * HID), F32),
        vmem((NODES, 2, both, HALF), BF16),
        vmem((MICRO, NODES, ROWS, CB), BF16),
        vmem((MICRO, NODES, ROWS, CB), BF16),
        vmem((MICRO, NODES, ROWS, CB), BF16),
        vmem((MICRO, ROWS, 2 * HID), BF16),
        vmem((DP, MICRO, ROWS, HID), BF16),
        vmem((DP, MICRO, ROWS, HID), BF16),
        vmem((MICRO, DP, ROWS, HID), BF16),
        vmem((MICRO, DP, 2, ROWS, CB), BF16),
        vmem((DP, 8, MICRO * ROWS), F32),
        vmem((DP, both, DB), BF16),
        vmem((DP, both, DB), BF16),
        vmem((NODES, DP, both, DB), BF16),
        vmem((DB, MICRO * ALL), BF16),
        vmem((HID, MICRO * ALL), BF16),
        vmem((MICRO, ALL, HID), BF16),
        vmem((MICRO, ALL, HID), BF16),
        vmem((HID, DB), BF16),
        vmem((both, WIDTH), BF16),
        vmem((both, WIDTH), BF16),
        vmem((NODES, NODES, OWN, CB), F32),
        vmem((MICRO, NODES - 1, 2, 16, 2 * CB), BF16),
        vmem((MICRO, NODES, 2, 16, 2 * CB), BF16),
        dma((8,)),
        dma((NODES,)),
        dma((2 * NODES,)),
        dma((9,)),
        dma((NODES,)),
        dma((NODES, 2)),
        dma((MICRO, NODES)),
        dma((MICRO, NODES)),
        dma((MICRO, NODES)),
        dma((MICRO, NODES)),
        dma((DP,)),
        dma((DP,)),
        dma((DP,)),
        dma((DP,)),
        dma((DP,)),
        dma((DP,)),
        dma((NODES,)),
        dma((NODES,)),
        dma((DP,)),
        dma((DP,)),
        dma((MICRO, DP)),
        dma((MICRO, DP)),
        dma((MICRO, DP)),
        dma((MICRO, DP)),
        dma((1,)),
        dma((1,)),
        dma((MICRO, NODES, 2)),
        dma((MICRO, NODES, 2)),
    ]
    anywhere = pl.BlockSpec(memory_space=pl.ANY)
    left = pl.pallas_call(
        body,
        out_shape=(
            jax.ShapeDtypeStruct((both, WIDTH), BF16),
            jax.ShapeDtypeStruct((DB, MICRO * ALL), BF16),
            jax.ShapeDtypeStruct((MICRO, ALL, HID), BF16),
            jax.ShapeDtypeStruct((MICRO, ALL, HID), BF16),
            jax.ShapeDtypeStruct((HID, DB), BF16),
        ),
        in_specs=[anywhere] * 9,
        out_specs=(anywhere,) * 5,
        scratch_shapes=scratch,
        compiler_params=pltpu.CompilerParams(
            collective_id=0, has_side_effects=True, vmem_limit_bytes=62 * 2**20
        ),
        cost_estimate=pl.CostEstimate(flops=5 * 10**9, bytes_accessed=24 * 10**6, transcendentals=10**6),
        name="relay",
    )(
        grad_out.reshape(both, WIDTH),
        layer_in.reshape(both, WIDTH),
        gate_pre[0],
        up_pre[0],
        expert_ids[0].transpose(0, 2, 1),
        route_weight[0].transpose(0, 2, 1),
        w_gate[0],
        w_up[0],
        w_down[0],
    )
    grad_in, g_gate, g_up, g_down = pl.pallas_call(
        finish,
        out_shape=(
            jax.ShapeDtypeStruct((both, WIDTH), BF16),
            jax.ShapeDtypeStruct((DB, HID), BF16),
            jax.ShapeDtypeStruct((DB, HID), BF16),
            jax.ShapeDtypeStruct((HID, DB), BF16),
        ),
        in_specs=[anywhere] * 5,
        out_specs=(anywhere,) * 4,
        scratch_shapes=[
            vmem((both, WIDTH), BF16),
            vmem((DB, MICRO * ALL), BF16),
            vmem((MICRO, ALL, HID), BF16),
            vmem((MICRO, ALL, HID), BF16),
            vmem((HID, DB), BF16),
            vmem((DB, HID), BF16),
            vmem((DB, HID), BF16),
            dma((13,)),
        ],
        compiler_params=pltpu.CompilerParams(vmem_limit_bytes=62 * 2**20),
        cost_estimate=pl.CostEstimate(flops=16 * 10**8, bytes_accessed=10**7, transcendentals=0),
        name="finish",
    )(*left)
    return grad_in.reshape(1, MICRO, OWN, WIDTH), g_gate[None], g_up[None], g_down[None]


def solution(mesh):
    return jax.shard_map(
        shards,
        mesh=mesh,
        in_specs=(
            P(None, ("dp", "node"), None),
            P("section", None, ("dp", "node"), None),
            P("section", None, "dp", "node"),
            P("section", None, "dp", "node"),
            P("section", None, "dp", None),
            P("section", None, "dp", None),
            P("section", None, "node"),
            P("section", None, "node"),
            P("section", "node", None),
        ),
        out_specs=(
            P("section", None, ("dp", "node"), None),
            P("section", "dp", "node"),
            P("section", "dp", "node"),
            P("section", "node", "dp"),
        ),
        check_vma=False,
    )
```

```python
import jax
import jax.numpy as jnp
from jax import lax
from jax.experimental import pallas as pl
from jax.experimental.pallas import tpu as pltpu
from jax.sharding import PartitionSpec as P

MESH = pl.DeviceIdType.MESH
F32 = jnp.float32
BF16 = jnp.bfloat16
SECTIONS = 4
DP = 4
NODES = 8
MICRO = 2
OWN = 8
ROWS = OWN * NODES
ALL = ROWS * DP
WIDTH = 3072
HID = 1024
CB = WIDTH // NODES
DB = WIDTH // DP
HALF = WIDTH // 2
RING = 12
WINDOW = 10
PIECES = 3 * NODES
OFFSETS = ((1, 2), (1, 1), (1, 3), (1, 0), (0, 2), (0, 1), (0, 3))


def near(n, offset):
    high, x = lax.div(n, 4), lax.rem(n, 4)
    return lax.rem(high + offset[0], 2) * 4 + lax.rem(x + offset[1], 4)


def dot(a, b):
    return lax.dot_general(a, b, (((1,), (0,)), ((), ())), preferred_element_type=F32)


def remote(src, dst, send, recv, **device):
    return pltpu.make_async_remote_copy(
        src_ref=src,
        dst_ref=dst,
        send_sem=send,
        recv_sem=recv,
        device_id=device,
        device_id_type=MESH,
    )


def body(
    grad_out, layer_in, gate_pre, up_pre, ids, route, w_gate, w_up, w_down,
    grad_in, lin_t, dga, dua, gd,
    wd_raw, wg_raw, wdt, wgut,
    ids_v, route_v, lin_v, coef_v, factors,
    go, dyg, prt, snd, dgu,
    gates, ups, backs, dys, crow,
    lsc, lx, lg, hid_t,
    ret, gi, fp, fs, fr,
    s_small, s_wd, s_wg,
    ss_go, rs_go, ss_sc, rs_sc, ss_ga, rs_ga,
    ss_gate, rs_gate, ss_up, rs_up, ss_lx, rs_lx, ss_lg, rs_lg,
    ss_cr, rs_cr, ss_b, rs_b, ss_dy, rs_dy, ss_ret, rs_ret, ss_f, rs_f,
):
    s = lax.axis_index("section")
    r = lax.axis_index("dp")
    n = lax.axis_index("node")
    above = lax.rem(s + 1, SECTIONS)
    below = lax.rem(s + SECTIONS - 1, SECTIONS)

    def peer(k):
        return lax.rem(r + k, DP)

    def load(i):
        if i < NODES:
            return pltpu.make_async_copy(
                w_down.at[pl.ds(i * (HID // NODES), HID // NODES), :], wd_raw.at[i], s_wd.at[i]
            )
        j = i - NODES
        ref = w_gate if j % 2 == 0 else w_up
        return pltpu.make_async_copy(
            ref.at[pl.ds((j // 2) * CB, CB), :], wg_raw.at[j % RING], s_wg.at[j]
        )

    def turn(i):
        load(i).wait()
        if i + WINDOW < PIECES:
            load(i + WINDOW).start()
        if i < NODES:
            rows = slice(i * (HID // NODES), (i + 1) * (HID // NODES))
            for j in range(NODES):
                wdt[j, :, rows] = wd_raw[i, :, j * CB : (j + 1) * CB].T
        else:
            j = i - NODES
            start = (j % 2) * HID
            wgut[j // 2, start : start + HID, :] = wg_raw[j % RING].T

    small = [
        pltpu.make_async_copy(ids, ids_v, s_small.at[0]),
        pltpu.make_async_copy(route, route_v, s_small.at[1]),
        pltpu.make_async_copy(layer_in, lin_v, s_small.at[2]),
        pltpu.make_async_copy(gate_pre, gates.at[r], s_small.at[3]),
        pltpu.make_async_copy(up_pre, ups.at[r], s_small.at[4]),
        pltpu.make_async_copy(grad_out.at[:, :HALF], go.at[n, 0], s_small.at[5]),
        pltpu.make_async_copy(grad_out.at[:, HALF:], go.at[n, 1], s_small.at[6]),
    ]
    for copy in small:
        copy.start()
    for i in range(WINDOW):
        load(i).start()

    barrier = pltpu.get_barrier_semaphore()
    for offset in OFFSETS:
        pl.semaphore_signal(
            barrier, inc=1, device_id={"node": near(n, offset)}, device_id_type=MESH
        )
    for k in range(1, DP):
        pl.semaphore_signal(barrier, inc=1, device_id={"dp": peer(k)}, device_id_type=MESH)

    @pl.when(s < SECTIONS - 1)
    def _():
        for j in range(NODES):
            pl.semaphore_signal(
                barrier, inc=1, device_id={"section": above, "node": j}, device_id_type=MESH
            )

    @pl.when(s > 0)
    def _():
        for j in range(NODES):
            pl.semaphore_signal(
                barrier, inc=1, device_id={"section": below, "node": j}, device_id_type=MESH
            )

    far = lax.rem(s + 2, SECTIONS)

    @pl.when(lax.rem(s, 2) == 1)
    def _():
        for offset in OFFSETS:
            pl.semaphore_signal(
                barrier,
                inc=1,
                device_id={"section": far, "node": near(n, offset)},
                device_id_type=MESH,
            )

    for copy in small:
        copy.wait()
    diagonal = lax.broadcasted_iota(jnp.int32, (ROWS, ROWS), 0) == lax.broadcasted_iota(
        jnp.int32, (ROWS, ROWS), 1
    )
    for m in range(MICRO):
        across = jnp.sum(
            jnp.where(ids_v[m] == 0, route_v[m], jnp.float32(0.0)), axis=0, keepdims=True
        )
        crow[r, 0:1, m * ROWS : (m + 1) * ROWS] = across
        coef_v[m * ROWS : (m + 1) * ROWS, :] = jnp.sum(
            jnp.where(diagonal, across, jnp.float32(0.0)), axis=1, keepdims=True
        )

    for i in range(NODES):
        turn(i)

    neighbours = jnp.minimum(s, 1) + jnp.minimum(SECTIONS - 1 - s, 1)
    pl.semaphore_wait(
        barrier,
        NODES - 1 + DP - 1 + neighbours * NODES + lax.rem(s, 2) * (NODES - 1),
    )

    def send_go(q, half):
        return remote(
            go.at[n, half], go.at[n, half], ss_go.at[q], rs_go.at[n, half],
            section=SECTIONS - 1, node=near(n, OFFSETS[q]),
        )

    def send_gate(k):
        return remote(gates.at[r], gates.at[r], ss_gate.at[k], rs_gate.at[r], dp=peer(k))

    def send_up(k):
        return remote(ups.at[r], ups.at[r], ss_up.at[k], rs_up.at[r], dp=peer(k))

    def send_lx(k):
        return remote(
            lsc.at[peer(k)], lx.at[r], ss_lx.at[k], rs_lx.at[r], dp=peer(k)
        )

    def send_cr(k):
        return remote(crow.at[r], crow.at[r], ss_cr.at[k], rs_cr.at[r], dp=peer(k))

    def send_lg(q):
        return remote(lx, lg.at[n], ss_lg.at[q], rs_lg.at[n], node=near(n, OFFSETS[q]))

    @pl.when(s == SECTIONS - 1)
    def _():
        for q in range(NODES - 1):
            send_go(q, 0).start()

    @pl.when(s == 1)
    def _():
        for q in range(NODES - 1):
            send_go(q, 1).start()

    for m in range(MICRO):
        gate = gates[r, m].astype(F32)
        active = jax.nn.sigmoid(gate) * coef_v[m * ROWS : (m + 1) * ROWS, :]
        factors[m, :, :HID] = (
            ups[r, m].astype(F32) * active * (1.0 + gate * (1.0 - jax.nn.sigmoid(gate)))
        )
        factors[m, :, HID:] = gate * active

    def exchange():
        scale = jnp.concatenate(
            [
                coef_v[pl.ds(pl.multiple_of(m * ROWS + n * OWN, OWN), OWN), :]
                for m in range(MICRO)
            ],
            axis=0,
        )
        for j in range(DP):
            lsc[j] = (lin_v[:, j * DB : (j + 1) * DB].astype(F32) * scale).astype(BF16)
        lx[r] = lsc[r]
        for k in range(1, DP):
            send_cr(k).start()
            send_lx(k).start()
        for k in range(1, DP):
            send_gate(k).start()
        for k in range(1, DP):
            send_up(k).start()

    def take_gates():
        for k in range(1, DP):
            j = peer(k)
            remote(gates.at[r], gates.at[j], ss_gate.at[k], rs_gate.at[j], dp=j).wait_recv()

    def prepare_hidden():
        for k in range(1, DP):
            j = peer(k)
            remote(ups.at[r], ups.at[j], ss_up.at[k], rs_up.at[j], dp=j).wait_recv()
            remote(crow.at[r], crow.at[j], ss_cr.at[k], rs_cr.at[j], dp=j).wait_recv()
        for m in range(MICRO):
            for c in range(2):
                pair = slice(2 * c, 2 * c + 2)
                g = gates[pair, m].reshape(2 * ROWS, HID).astype(F32)
                u = ups[pair, m].reshape(2 * ROWS, HID).astype(F32)
                hidden = (g * jax.nn.sigmoid(g) * u).astype(BF16)
                across = jnp.concatenate(
                    [crow[2 * c + i, 0:1, m * ROWS : (m + 1) * ROWS] for i in range(2)], axis=1
                )
                hid_t[:, m * ALL + c * 128 : m * ALL + (c + 1) * 128] = (
                    hidden.T.astype(F32) * across
                ).astype(BF16)

    def gather_inputs():
        for k in range(1, DP):
            remote(lsc.at[0], lx.at[peer(k)], ss_lx.at[k], rs_lx.at[peer(k)], dp=peer(k)).wait_recv()
        lg[n] = lx[...]
        for q in range(NODES - 1):
            send_lg(q).start()

    def prepare_inputs():
        for offset in OFFSETS:
            j = near(n, offset)
            remote(lx, lg.at[j], ss_lg.at[0], rs_lg.at[j], node=j).wait_recv()
        for m in range(MICRO):
            rows = jnp.concatenate(
                [
                    lg[i, k, :, :].astype(F32)[m * OWN : (m + 1) * OWN]
                    for k in range(DP)
                    for i in range(NODES)
                ],
                axis=0,
            )
            lin_t[:, m * ALL : (m + 1) * ALL] = rows.astype(BF16).T

    @pl.when(s < 2)
    def _():
        exchange()

    for i in range(NODES, PIECES):
        turn(i)

    @pl.when(s < 2)
    def _():
        gather_inputs()
        take_gates()

    @pl.when(s == 0)
    def _():
        prepare_hidden()
        prepare_inputs()

    def send_ga(m, q):
        return remote(
            dyg.at[m, n], dyg.at[m, n], ss_ga.at[m, q], rs_ga.at[m, n], node=near(n, OFFSETS[q])
        )

    def recv_ga(m, j):
        return remote(dyg.at[m, j], dyg.at[m, j], ss_ga.at[m, 0], rs_ga.at[m, j], node=j)

    def finish_back(m, back):
        backs[m, r] = back.astype(BF16)
        dgu[m, :, :HID] = (back * factors[m, :, :HID]).astype(BF16)
        dgu[m, :, HID:] = (back * factors[m, :, HID:]).astype(BF16)

    def unpack(m, half, columns):
        block = go[:, half, :, columns].astype(F32)
        return block[:, m * OWN : (m + 1) * OWN, :].reshape(ROWS, CB).astype(BF16)

    @pl.when(s == SECTIONS - 1)
    def _():
        for half in range(2):
            for offset in OFFSETS:
                j = near(n, offset)
                remote(
                    go.at[n, half], go.at[j, half], ss_go.at[0], rs_go.at[j, half],
                    section=SECTIONS - 1, node=j,
                ).wait_recv()
        back = jnp.zeros((MICRO * ROWS, HID), F32)
        for j in range(NODES):
            start = (j % 4) * CB
            block = go[:, j // 4, :, start : start + CB].reshape(MICRO * ROWS, CB)
            back = back + dot(block, wdt[j])
        back = back.reshape(NODES, MICRO * OWN, HID)
        for m in range(MICRO):
            finish_back(m, back[:, m * OWN : (m + 1) * OWN, :].reshape(ROWS, HID))
            dyg[m, n] = unpack(m, lax.div(n, 4), pl.ds(pl.multiple_of(lax.rem(n, 4) * CB, CB), CB))

    @pl.when(s < SECTIONS - 1)
    def _():
        for m in range(MICRO):
            for j in range(NODES):
                remote(
                    snd.at[m, j], prt.at[m, j], ss_sc.at[m, j], rs_sc.at[m, j],
                    section=above, node=j,
                ).wait_recv()
            total = prt[m, 0].astype(F32)
            for j in range(1, NODES):
                total = total + prt[m, j].astype(F32)
            dyg[m, n] = total.astype(BF16)
            for q in range(NODES - 1):
                send_ga(m, q).start()

    def send_sc(m, j):
        return remote(
            snd.at[m, j], prt.at[m, n], ss_sc.at[m, j], rs_sc.at[m, n], section=below, node=j
        )

    def send_b(m, k):
        return remote(backs.at[m, r], backs.at[m, r], ss_b.at[m, k], rs_b.at[m, r], dp=peer(k))

    def send_dy(m, k):
        return remote(
            dyg.at[m, pl.ds(2 * peer(k), 2)], dys.at[m, r], ss_dy.at[m, k], rs_dy.at[m, r],
            dp=peer(k),
        )

    def send_f(m, q, step):
        half = (1 - lax.div(n, 4)) if step == 0 else lax.div(n, 4)
        return remote(
            fs.at[m, q, step], fr.at[m, n, half], ss_f.at[m, q, step], rs_f.at[m, n, half],
            node=near(n, OFFSETS[q]),
        )

    def send_tokens(m, step):
        half = (1 - lax.div(n, 4)) if step == 0 else lax.div(n, 4)

        def put(place, i):
            for c in range(2):
                place[:, c * CB : (c + 1) * CB] = jnp.concatenate(
                    [fp[half * 4 + c, i], fp[half * 4 + 2 + c, i]], axis=0
                ).astype(BF16)

        for q in range(NODES - 1):
            put(fs.at[m, q, step], near(n, OFFSETS[q]))
            send_f(m, q, step).start()
        put(fr.at[m, n, half], n)

    def exchange_dy(m):
        for k in range(1, DP):
            send_dy(m, k).start()
        dys[m, r] = dyg[m, pl.ds(2 * r, 2)]

    def exchange_back(m):
        for k in range(1, DP):
            send_b(m, k).start()

    arrivals = (((0, 1), (0, 3)), ((0, 2), (1, 0)), ((1, 1), (1, 3), (1, 2)))
    order = OFFSETS + ((0, 0),)
    for m in range(MICRO):

        @pl.when(s < SECTIONS - 1)
        def _():
            back = dot(dyg[m, n], wdt[n])
            for group in arrivals:
                for offset in group:
                    recv_ga(m, near(n, offset)).wait_recv()
                if group is arrivals[-1]:

                    @pl.when(s == 0)
                    def _():
                        exchange_dy(m)

                for offset in group:
                    j = near(n, offset)
                    back = back + dot(dyg[m, j], wdt[j])
            finish_back(m, back)

        @pl.when(s == 0)
        def _():
            exchange_back(m)

        for g in range(NODES // 2):
            for offset in order[2 * g : 2 * g + 2]:
                j = near(n, offset)
                part = dot(dgu[m], wgut[j])
                if offset == (0, 0):
                    part = part + dyg[m, n].astype(F32)
                snd[m, j] = part.astype(BF16)
                fp[j] = part.reshape(NODES, OWN, CB)

            @pl.when(s > 0)
            def _():
                for offset in order[2 * g : 2 * g + 2]:
                    send_sc(m, near(n, offset)).start()

            if g % 2 == 1:

                @pl.when(s == 0)
                def _():
                    send_tokens(m, g // 2)

        @pl.when(jnp.logical_and(s > 0, s < SECTIONS - 1))
        def _():
            exchange_back(m)
            exchange_dy(m)

    @pl.when(s == SECTIONS - 1)
    def _():
        for m in range(MICRO):
            for j in range(NODES):
                start = (j % 4) * CB
                dyg[m, j] = unpack(m, j // 4, slice(start, start + CB))

        for m in range(MICRO):
            exchange_back(m)
            exchange_dy(m)

    def send_ret():
        return remote(ret, gi, ss_ret.at[0], rs_ret.at[0], section=above)

    @pl.when(s < SECTIONS - 1)
    def _():
        window = pl.ds(pl.multiple_of(lax.div(n, 2) * 16, 16), 16)
        odd = lax.rem(n, 2) == 1
        for j in range(NODES):
            picked = []
            for m in range(MICRO):
                value = dyg[m, j, window, :].astype(F32)
                picked.append(jnp.where(odd, value[OWN:], value[:OWN]))
            ret[:, j * CB : (j + 1) * CB] = jnp.concatenate(picked, axis=0).astype(BF16)
        send_ret().start()

    @pl.when(s >= 2)
    def _():
        exchange()

    @pl.when(s == 2)
    def _():
        gather_inputs()

    @pl.when(s >= 2)
    def _():
        take_gates()

    @pl.when(s > 0)
    def _():
        prepare_hidden()

    def take_ret():
        remote(ret, gi, ss_ret.at[0], rs_ret.at[0], section=below).wait_recv()

    @pl.when(s == SECTIONS - 1)
    def _():
        take_ret()
        gather_inputs()

    @pl.when(s > 0)
    def _():
        prepare_inputs()

    def spread(m):
        for k in range(1, DP):
            j = peer(k)
            remote(backs.at[m, r], backs.at[m, j], ss_b.at[m, k], rs_b.at[m, j], dp=j).wait_recv()
        for k in range(DP):
            rows = slice(k * ROWS, (k + 1) * ROWS)
            back = backs[m, k].astype(F32)
            gate = gates[k, m].astype(F32)
            sigma = jax.nn.sigmoid(gate)
            dga[m, rows, :] = (
                back * ups[k, m].astype(F32) * sigma * (1.0 + gate * (1.0 - sigma))
            ).astype(BF16)
            dua[m, rows, :] = (back * gate * sigma).astype(BF16)

    spread(0)
    for m in range(MICRO):
        for k in range(1, DP):
            j = peer(k)
            remote(
                dyg.at[m, pl.ds(0, 2)], dys.at[m, j], ss_dy.at[m, k], rs_dy.at[m, j], dp=j
            ).wait_recv()
    for i in range(HID // 256):
        rows = slice(i * 256, (i + 1) * 256)
        for h in range(2):
            value = dot(hid_t[rows, :ALL], dys[0, :, h].reshape(ALL, CB))
            value = value + dot(hid_t[rows, ALL:], dys[1, :, h].reshape(ALL, CB))
            gd[rows, h * CB : (h + 1) * CB] = value.astype(BF16)

    @pl.when(s == 0)
    def _():
        for m in range(MICRO):
            for offset in OFFSETS:
                j = near(n, offset)
                for half in range(2):
                    remote(
                        fs.at[m, 0, half], fr.at[m, j, half], ss_f.at[m, 0, half],
                        rs_f.at[m, j, half], node=j,
                    ).wait_recv()
        for half in range(2):
            totals = []
            for m in range(MICRO):
                total = fr[m, 0, half].astype(F32)
                for j in range(1, NODES):
                    total = total + fr[m, j, half].astype(F32)
                totals.append(total)
            for c in range(2):
                start = half * HALF + c * 2 * CB
                gi[:, start : start + 2 * CB] = jnp.concatenate(
                    [total[c * OWN : (c + 1) * OWN] for total in totals], axis=0
                ).astype(BF16)

    @pl.when(jnp.logical_and(s > 0, s < SECTIONS - 1))
    def _():
        take_ret()

    grad_in[...] = gi[...]
    spread(1)

    @pl.when(s == SECTIONS - 1)
    def _():
        for q in range(NODES - 1):
            send_go(q, 0).wait_send()

    @pl.when(s == 1)
    def _():
        for q in range(NODES - 1):
            send_go(q, 1).wait_send()

    for k in range(1, DP):
        send_gate(k).wait_send()
        send_up(k).wait_send()
        send_lx(k).wait_send()
        send_cr(k).wait_send()
    for q in range(NODES - 1):
        send_lg(q).wait_send()
    for m in range(MICRO):
        for k in range(1, DP):
            send_b(m, k).wait_send()
            send_dy(m, k).wait_send()

    @pl.when(s < SECTIONS - 1)
    def _():
        for m in range(MICRO):
            for q in range(NODES - 1):
                send_ga(m, q).wait_send()
        send_ret().wait_send()

    @pl.when(s > 0)
    def _():
        for m in range(MICRO):
            for j in range(NODES):
                send_sc(m, j).wait_send()

    @pl.when(s == 0)
    def _():
        for m in range(MICRO):
            for q in range(NODES - 1):
                for step in range(2):
                    send_f(m, q, step).wait_send()


def finish(
    grad_in, lin, dg, du, down,
    o_in, o_gate, o_up, o_down,
    gate_v, up_v, sems,
):
    stores = [
        pltpu.make_async_copy(down, o_down, sems.at[0]),
        pltpu.make_async_copy(grad_in, o_in, sems.at[1]),
    ]
    for copy in stores:
        copy.start()
    for which, (d, staged, out) in enumerate(((dg, gate_v, o_gate), (du, up_v, o_up))):
        for i in range(DB // 256):
            rows = pl.ds(i * 256, 256)
            value = dot(lin[rows, :ALL], d[0]) + dot(lin[rows, ALL:], d[1])
            staged[rows, :] = value.astype(BF16)
            stores.append(
                pltpu.make_async_copy(
                    staged.at[rows, :], out.at[rows, :], sems.at[2 + 3 * which + i]
                )
            )
            stores[-1].start()
    for copy in stores:
        copy.wait()


def shards(grad_out, layer_in, gate_pre, up_pre, expert_ids, route_weight, w_gate, w_up, w_down):
    both = MICRO * OWN
    dma = pltpu.SemaphoreType.DMA
    vmem = pltpu.VMEM
    scratch = [
        vmem((NODES, HID // NODES, WIDTH), BF16),
        vmem((RING, CB, HID), BF16),
        vmem((NODES, CB, HID), BF16),
        vmem((NODES, 2 * HID, CB), BF16),
        vmem((MICRO, 2, ROWS), jnp.int32),
        vmem((MICRO, 2, ROWS), F32),
        vmem((both, WIDTH), BF16),
        vmem((MICRO * ROWS, 1), F32),
        vmem((MICRO, ROWS, 2 * HID), F32),
        vmem((NODES, 2, both, HALF), BF16),
        vmem((MICRO, NODES, ROWS, CB), BF16),
        vmem((MICRO, NODES, ROWS, CB), BF16),
        vmem((MICRO, NODES, ROWS, CB), BF16),
        vmem((MICRO, ROWS, 2 * HID), BF16),
        vmem((DP, MICRO, ROWS, HID), BF16),
        vmem((DP, MICRO, ROWS, HID), BF16),
        vmem((MICRO, DP, ROWS, HID), BF16),
        vmem((MICRO, DP, 2, ROWS, CB), BF16),
        vmem((DP, 8, MICRO * ROWS), F32),
        vmem((DP, both, DB), BF16),
        vmem((DP, both, DB), BF16),
        vmem((NODES, DP, both, DB), BF16),
        vmem((HID, MICRO * ALL), BF16),
        vmem((both, WIDTH), BF16),
        vmem((both, WIDTH), BF16),
        vmem((NODES, NODES, OWN, CB), F32),
        vmem((MICRO, NODES - 1, 2, 16, 2 * CB), BF16),
        vmem((MICRO, NODES, 2, 16, 2 * CB), BF16),
        dma((8,)),
        dma((NODES,)),
        dma((2 * NODES,)),
        dma((NODES,)),
        dma((NODES, 2)),
        dma((MICRO, NODES)),
        dma((MICRO, NODES)),
        dma((MICRO, NODES)),
        dma((MICRO, NODES)),
        dma((DP,)),
        dma((DP,)),
        dma((DP,)),
        dma((DP,)),
        dma((DP,)),
        dma((DP,)),
        dma((NODES,)),
        dma((NODES,)),
        dma((DP,)),
        dma((DP,)),
        dma((MICRO, DP)),
        dma((MICRO, DP)),
        dma((MICRO, DP)),
        dma((MICRO, DP)),
        dma((1,)),
        dma((1,)),
        dma((MICRO, NODES, 2)),
        dma((MICRO, NODES, 2)),
    ]
    anywhere = pl.BlockSpec(memory_space=pl.ANY)
    inside = pl.BlockSpec(memory_space=pltpu.VMEM)
    left = pl.pallas_call(
        body,
        out_shape=(
            vmem((both, WIDTH), BF16),
            vmem((DB, MICRO * ALL), BF16),
            vmem((MICRO, ALL, HID), BF16),
            vmem((MICRO, ALL, HID), BF16),
            vmem((HID, DB), BF16),
        ),
        in_specs=[anywhere] * 9,
        out_specs=(inside,) * 5,
        scratch_shapes=scratch,
        compiler_params=pltpu.CompilerParams(
            collective_id=0, has_side_effects=True, vmem_limit_bytes=53 * 2**20
        ),
        cost_estimate=pl.CostEstimate(flops=5 * 10**9, bytes_accessed=24 * 10**6, transcendentals=10**6),
        name="relay",
    )(
        grad_out.reshape(both, WIDTH),
        layer_in.reshape(both, WIDTH),
        gate_pre[0],
        up_pre[0],
        expert_ids[0].transpose(0, 2, 1),
        route_weight[0].transpose(0, 2, 1),
        w_gate[0],
        w_up[0],
        w_down[0],
    )
    grad_in, g_gate, g_up, g_down = pl.pallas_call(
        finish,
        out_shape=(
            jax.ShapeDtypeStruct((both, WIDTH), BF16),
            jax.ShapeDtypeStruct((DB, HID), BF16),
            jax.ShapeDtypeStruct((DB, HID), BF16),
            jax.ShapeDtypeStruct((HID, DB), BF16),
        ),
        in_specs=[inside] * 5,
        out_specs=(anywhere,) * 4,
        scratch_shapes=[
            vmem((DB, HID), BF16),
            vmem((DB, HID), BF16),
            dma((8,)),
        ],
        compiler_params=pltpu.CompilerParams(vmem_limit_bytes=30 * 2**20),
        cost_estimate=pl.CostEstimate(flops=16 * 10**8, bytes_accessed=10**7, transcendentals=0),
        name="finish",
    )(*(pltpu.with_memory_space_constraint(x, pltpu.VMEM) for x in left))
    return grad_in.reshape(1, MICRO, OWN, WIDTH), g_gate[None], g_up[None], g_down[None]


def solution(mesh):
    return jax.shard_map(
        shards,
        mesh=mesh,
        in_specs=(
            P(None, ("dp", "node"), None),
            P("section", None, ("dp", "node"), None),
            P("section", None, "dp", "node"),
            P("section", None, "dp", "node"),
            P("section", None, "dp", None),
            P("section", None, "dp", None),
            P("section", None, "node"),
            P("section", None, "node"),
            P("section", "node", None),
        ),
        out_specs=(
            P("section", None, ("dp", "node"), None),
            P("section", "dp", "node"),
            P("section", "dp", "node"),
            P("section", "node", "dp"),
        ),
        check_vma=False,
    )
```

```python
import jax
import jax.numpy as jnp
from jax import lax
from jax.experimental import pallas as pl
from jax.experimental.pallas import tpu as pltpu
from jax.sharding import PartitionSpec as P

MESH = pl.DeviceIdType.MESH
F32 = jnp.float32
BF16 = jnp.bfloat16
SECTIONS = 4
DP = 4
NODES = 8
MICRO = 2
OWN = 8
ROWS = OWN * NODES
ALL = ROWS * DP
WIDTH = 3072
HID = 1024
CB = WIDTH // NODES
DB = WIDTH // DP
HALF = WIDTH // 2
RING = 12
WINDOW = 10
PIECES = 3 * NODES
OFFSETS = ((1, 2), (1, 1), (1, 3), (1, 0), (0, 2), (0, 1), (0, 3))


def near(n, offset):
    high, x = lax.div(n, 4), lax.rem(n, 4)
    return lax.rem(high + offset[0], 2) * 4 + lax.rem(x + offset[1], 4)


def dot(a, b):
    return lax.dot_general(a, b, (((1,), (0,)), ((), ())), preferred_element_type=F32)


def remote(src, dst, send, recv, **device):
    return pltpu.make_async_remote_copy(
        src_ref=src,
        dst_ref=dst,
        send_sem=send,
        recv_sem=recv,
        device_id=device,
        device_id_type=MESH,
    )


def body(
    grad_out, layer_in, gate_pre, up_pre, ids, route, w_gate, w_up, w_down,
    grad_in, lin_t, dga, dua, gd,
    wd_raw, wg_raw, wdt, wgut,
    ids_v, route_v, lin_v, coef_v, factors,
    go, dyg, prt, snd, dgu,
    gates, ups, backs, dys, crow,
    lsc, lx, lg, hid_t,
    ret, gi, fp, fs, fr,
    s_small, s_wd, s_wg,
    ss_go, rs_go, ss_sc, rs_sc, ss_ga, rs_ga,
    ss_gate, rs_gate, ss_up, rs_up, ss_lx, rs_lx, ss_lg, rs_lg,
    ss_fw, rs_fw, ss_cr, rs_cr, ss_b, rs_b, ss_dy, rs_dy, ss_ret, rs_ret, ss_f, rs_f,
):
    s = lax.axis_index("section")
    r = lax.axis_index("dp")
    n = lax.axis_index("node")
    above = lax.rem(s + 1, SECTIONS)
    below = lax.rem(s + SECTIONS - 1, SECTIONS)

    def peer(k):
        return lax.rem(r + k, DP)

    def load(i):
        if i < NODES:
            return pltpu.make_async_copy(
                w_down.at[pl.ds(i * (HID // NODES), HID // NODES), :], wd_raw.at[i], s_wd.at[i]
            )
        j = i - NODES
        ref = w_gate if j % 2 == 0 else w_up
        return pltpu.make_async_copy(
            ref.at[pl.ds((j // 2) * CB, CB), :], wg_raw.at[j % RING], s_wg.at[j]
        )

    def turn(i):
        load(i).wait()
        if i + WINDOW < PIECES:
            load(i + WINDOW).start()
        if i < NODES:
            rows = slice(i * (HID // NODES), (i + 1) * (HID // NODES))
            for j in range(NODES):
                wdt[j, :, rows] = wd_raw[i, :, j * CB : (j + 1) * CB].T
        else:
            j = i - NODES
            start = (j % 2) * HID
            wgut[j // 2, start : start + HID, :] = wg_raw[j % RING].T

    small = [
        pltpu.make_async_copy(ids, ids_v, s_small.at[0]),
        pltpu.make_async_copy(route, route_v, s_small.at[1]),
        pltpu.make_async_copy(layer_in, lin_v, s_small.at[2]),
        pltpu.make_async_copy(gate_pre, gates.at[r], s_small.at[3]),
        pltpu.make_async_copy(up_pre, ups.at[r], s_small.at[4]),
        pltpu.make_async_copy(grad_out.at[:, :HALF], go.at[n, 0], s_small.at[5]),
        pltpu.make_async_copy(grad_out.at[:, HALF:], go.at[n, 1], s_small.at[6]),
    ]
    for copy in small:
        copy.start()
    for i in range(WINDOW):
        load(i).start()

    barrier = pltpu.get_barrier_semaphore()
    for offset in OFFSETS:
        pl.semaphore_signal(
            barrier, inc=1, device_id={"node": near(n, offset)}, device_id_type=MESH
        )
    for k in range(1, DP):
        pl.semaphore_signal(barrier, inc=1, device_id={"dp": peer(k)}, device_id_type=MESH)

    @pl.when(s < SECTIONS - 1)
    def _():
        for j in range(NODES):
            pl.semaphore_signal(
                barrier, inc=1, device_id={"section": above, "node": j}, device_id_type=MESH
            )

    @pl.when(s > 0)
    def _():
        for j in range(NODES):
            pl.semaphore_signal(
                barrier, inc=1, device_id={"section": below, "node": j}, device_id_type=MESH
            )

    far = lax.rem(s + 2, SECTIONS)

    @pl.when(lax.rem(s, 2) == 1)
    def _():
        for offset in OFFSETS:
            pl.semaphore_signal(
                barrier,
                inc=1,
                device_id={"section": far, "node": near(n, offset)},
                device_id_type=MESH,
            )

    for copy in small:
        copy.wait()
    diagonal = lax.broadcasted_iota(jnp.int32, (ROWS, ROWS), 0) == lax.broadcasted_iota(
        jnp.int32, (ROWS, ROWS), 1
    )
    for m in range(MICRO):
        across = jnp.sum(
            jnp.where(ids_v[m] == 0, route_v[m], jnp.float32(0.0)), axis=0, keepdims=True
        )
        crow[r, 0:1, m * ROWS : (m + 1) * ROWS] = across
        coef_v[m * ROWS : (m + 1) * ROWS, :] = jnp.sum(
            jnp.where(diagonal, across, jnp.float32(0.0)), axis=1, keepdims=True
        )

    for i in range(NODES):
        turn(i)

    neighbours = jnp.minimum(s, 1) + jnp.minimum(SECTIONS - 1 - s, 1)
    pl.semaphore_wait(
        barrier,
        NODES - 1 + DP - 1 + neighbours * NODES + lax.rem(s, 2) * (NODES - 1),
    )

    def send_go(q, half):
        return remote(
            go.at[n, half], go.at[n, half], ss_go.at[q], rs_go.at[n, half],
            section=SECTIONS - 1, node=near(n, OFFSETS[q]),
        )

    def send_gate(k):
        return remote(gates.at[r], gates.at[r], ss_gate.at[k], rs_gate.at[r], dp=peer(k))

    def send_up(k):
        return remote(ups.at[r], ups.at[r], ss_up.at[k], rs_up.at[r], dp=peer(k))

    def forward(which, half):
        array = (gates, ups)[which]
        block = array.at[peer((DP - 1, 1)[half]), half]
        return remote(
            block, block, ss_fw.at[2 * which + half], rs_fw.at[2 * which + half],
            dp=peer((1, DP - 1)[half]),
        )

    def send_lx(k):
        return remote(
            lsc.at[peer(k)], lx.at[r], ss_lx.at[k], rs_lx.at[r], dp=peer(k)
        )

    def send_cr(k):
        return remote(crow.at[r], crow.at[r], ss_cr.at[k], rs_cr.at[r], dp=peer(k))

    def send_lg(q):
        return remote(lx, lg.at[n], ss_lg.at[q], rs_lg.at[n], node=near(n, OFFSETS[q]))

    @pl.when(s == SECTIONS - 1)
    def _():
        for q in range(NODES - 1):
            send_go(q, 0).start()

    @pl.when(s == 1)
    def _():
        for q in range(NODES - 1):
            send_go(q, 1).start()

    for m in range(MICRO):
        gate = gates[r, m].astype(F32)
        active = jax.nn.sigmoid(gate) * coef_v[m * ROWS : (m + 1) * ROWS, :]
        factors[m, :, :HID] = (
            ups[r, m].astype(F32) * active * (1.0 + gate * (1.0 - jax.nn.sigmoid(gate)))
        )
        factors[m, :, HID:] = gate * active

    def exchange():
        scale = jnp.concatenate(
            [
                coef_v[pl.ds(pl.multiple_of(m * ROWS + n * OWN, OWN), OWN), :]
                for m in range(MICRO)
            ],
            axis=0,
        )
        for j in range(DP):
            lsc[j] = (lin_v[:, j * DB : (j + 1) * DB].astype(F32) * scale).astype(BF16)
        lx[r] = lsc[r]
        for k in range(1, DP):
            send_cr(k).start()
            send_lx(k).start()
        for k in (1, DP - 1):
            send_gate(k).start()
        for k in (1, DP - 1):
            send_up(k).start()

    def take_gates():
        for k in (1, DP - 1):
            j = peer(k)
            remote(gates.at[r], gates.at[j], ss_gate.at[k], rs_gate.at[j], dp=j).wait_recv()
        for half in range(2):
            forward(0, half).start()
        for k in (1, DP - 1):
            j = peer(k)
            remote(ups.at[r], ups.at[j], ss_up.at[k], rs_up.at[j], dp=j).wait_recv()
        for half in range(2):
            forward(1, half).start()

    def prepare_hidden():
        for k in range(1, DP):
            j = peer(k)
            remote(crow.at[r], crow.at[j], ss_cr.at[k], rs_cr.at[j], dp=j).wait_recv()
        for which, array in enumerate((gates, ups)):
            for half in range(2):
                place = array.at[peer(2), half]
                i = 2 * which + half
                remote(place, place, ss_fw.at[i], rs_fw.at[i], dp=peer(1)).wait_recv()
        for m in range(MICRO):
            for c in range(2):
                pair = slice(2 * c, 2 * c + 2)
                g = gates[pair, m].reshape(2 * ROWS, HID).astype(F32)
                u = ups[pair, m].reshape(2 * ROWS, HID).astype(F32)
                hidden = (g * jax.nn.sigmoid(g) * u).astype(BF16)
                across = jnp.concatenate(
                    [crow[2 * c + i, 0:1, m * ROWS : (m + 1) * ROWS] for i in range(2)], axis=1
                )
                hid_t[:, m * ALL + c * 128 : m * ALL + (c + 1) * 128] = (
                    hidden.T.astype(F32) * across
                ).astype(BF16)

    def gather_inputs():
        for k in range(1, DP):
            remote(lsc.at[0], lx.at[peer(k)], ss_lx.at[k], rs_lx.at[peer(k)], dp=peer(k)).wait_recv()
        lg[n] = lx[...]
        for q in range(NODES - 1):
            send_lg(q).start()

    def prepare_inputs():
        for offset in OFFSETS:
            j = near(n, offset)
            remote(lx, lg.at[j], ss_lg.at[0], rs_lg.at[j], node=j).wait_recv()
        for m in range(MICRO):
            rows = jnp.concatenate(
                [
                    lg[i, k, :, :].astype(F32)[m * OWN : (m + 1) * OWN]
                    for k in range(DP)
                    for i in range(NODES)
                ],
                axis=0,
            )
            lin_t[:, m * ALL : (m + 1) * ALL] = rows.astype(BF16).T

    @pl.when(s < 2)
    def _():
        exchange()

    for i in range(NODES, PIECES):
        turn(i)

    @pl.when(s < 2)
    def _():
        gather_inputs()
        take_gates()

    @pl.when(s == 0)
    def _():
        prepare_hidden()
        prepare_inputs()

    def send_ga(m, q):
        return remote(
            dyg.at[m, n], dyg.at[m, n], ss_ga.at[m, q], rs_ga.at[m, n], node=near(n, OFFSETS[q])
        )

    def recv_ga(m, j):
        return remote(dyg.at[m, j], dyg.at[m, j], ss_ga.at[m, 0], rs_ga.at[m, j], node=j)

    def finish_back(m, back):
        backs[m, r] = back.astype(BF16)
        dgu[m, :, :HID] = (back * factors[m, :, :HID]).astype(BF16)
        dgu[m, :, HID:] = (back * factors[m, :, HID:]).astype(BF16)

    def unpack(m, half, columns):
        block = go[:, half, :, columns].astype(F32)
        return block[:, m * OWN : (m + 1) * OWN, :].reshape(ROWS, CB).astype(BF16)

    @pl.when(s == SECTIONS - 1)
    def _():
        for half in range(2):
            for offset in OFFSETS:
                j = near(n, offset)
                remote(
                    go.at[n, half], go.at[j, half], ss_go.at[0], rs_go.at[j, half],
                    section=SECTIONS - 1, node=j,
                ).wait_recv()
        back = jnp.zeros((MICRO * ROWS, HID), F32)
        for j in range(NODES):
            start = (j % 4) * CB
            block = go[:, j // 4, :, start : start + CB].reshape(MICRO * ROWS, CB)
            back = back + dot(block, wdt[j])
        back = back.reshape(NODES, MICRO * OWN, HID)
        for m in range(MICRO):
            finish_back(m, back[:, m * OWN : (m + 1) * OWN, :].reshape(ROWS, HID))
            dyg[m, n] = unpack(m, lax.div(n, 4), pl.ds(pl.multiple_of(lax.rem(n, 4) * CB, CB), CB))

    @pl.when(s < SECTIONS - 1)
    def _():
        for m in range(MICRO):
            for j in range(NODES):
                remote(
                    snd.at[m, j], prt.at[m, j], ss_sc.at[m, j], rs_sc.at[m, j],
                    section=above, node=j,
                ).wait_recv()
            total = prt[m, 0].astype(F32)
            for j in range(1, NODES):
                total = total + prt[m, j].astype(F32)
            dyg[m, n] = total.astype(BF16)
            for q in range(NODES - 1):
                send_ga(m, q).start()

    def send_sc(m, j):
        return remote(
            snd.at[m, j], prt.at[m, n], ss_sc.at[m, j], rs_sc.at[m, n], section=below, node=j
        )

    def send_b(m, k):
        return remote(backs.at[m, r], backs.at[m, r], ss_b.at[m, k], rs_b.at[m, r], dp=peer(k))

    def send_dy(m, k):
        return remote(
            dyg.at[m, pl.ds(2 * peer(k), 2)], dys.at[m, r], ss_dy.at[m, k], rs_dy.at[m, r],
            dp=peer(k),
        )

    def send_f(m, q, step):
        half = (1 - lax.div(n, 4)) if step == 0 else lax.div(n, 4)
        return remote(
            fs.at[m, q, step], fr.at[m, n, half], ss_f.at[m, q, step], rs_f.at[m, n, half],
            node=near(n, OFFSETS[q]),
        )

    def send_tokens(m, step):
        half = (1 - lax.div(n, 4)) if step == 0 else lax.div(n, 4)

        def put(place, i):
            for c in range(2):
                place[:, c * CB : (c + 1) * CB] = jnp.concatenate(
                    [fp[half * 4 + c, i], fp[half * 4 + 2 + c, i]], axis=0
                ).astype(BF16)

        for q in range(NODES - 1):
            put(fs.at[m, q, step], near(n, OFFSETS[q]))
            send_f(m, q, step).start()
        put(fr.at[m, n, half], n)

    def exchange_dy(m):
        for k in range(1, DP):
            send_dy(m, k).start()
        dys[m, r] = dyg[m, pl.ds(2 * r, 2)]

    def exchange_back(m):
        for k in range(1, DP):
            send_b(m, k).start()

    arrivals = (((0, 1), (0, 3)), ((0, 2), (1, 0)), ((1, 1), (1, 3), (1, 2)))
    order = OFFSETS + ((0, 0),)
    for m in range(MICRO):

        @pl.when(s < SECTIONS - 1)
        def _():
            back = dot(dyg[m, n], wdt[n])
            for group in arrivals:
                for offset in group:
                    recv_ga(m, near(n, offset)).wait_recv()
                if group is arrivals[-1]:

                    @pl.when(s == 0)
                    def _():
                        exchange_dy(m)

                for offset in group:
                    j = near(n, offset)
                    back = back + dot(dyg[m, j], wdt[j])
            finish_back(m, back)

        @pl.when(s == 0)
        def _():
            exchange_back(m)

        for g in range(2):
            for offset in order[4 * g : 4 * g + 4]:
                j = near(n, offset)
                part = dot(dgu[m], wgut[j])
                if offset == (0, 0):
                    part = part + dyg[m, n].astype(F32)
                snd[m, j] = part.astype(BF16)
                fp[j] = part.reshape(NODES, OWN, CB)

            @pl.when(s > 0)
            def _():
                for offset in order[4 * g : 4 * g + 4]:
                    send_sc(m, near(n, offset)).start()

            if True:

                @pl.when(s == 0)
                def _():
                    send_tokens(m, g)

        @pl.when(jnp.logical_and(s > 0, s < SECTIONS - 1))
        def _():
            exchange_back(m)
            exchange_dy(m)

    @pl.when(s == SECTIONS - 1)
    def _():
        for m in range(MICRO):
            for j in range(NODES):
                start = (j % 4) * CB
                dyg[m, j] = unpack(m, j // 4, slice(start, start + CB))

        for m in range(MICRO):
            exchange_back(m)
            exchange_dy(m)

    def send_ret():
        return remote(ret, gi, ss_ret.at[0], rs_ret.at[0], section=above)

    @pl.when(s < SECTIONS - 1)
    def _():
        window = pl.ds(pl.multiple_of(lax.div(n, 2) * 16, 16), 16)
        odd = lax.rem(n, 2) == 1
        for j in range(NODES):
            picked = []
            for m in range(MICRO):
                value = dyg[m, j, window, :].astype(F32)
                picked.append(jnp.where(odd, value[OWN:], value[:OWN]))
            ret[:, j * CB : (j + 1) * CB] = jnp.concatenate(picked, axis=0).astype(BF16)
        send_ret().start()

    @pl.when(s >= 2)
    def _():
        exchange()

    @pl.when(s == 2)
    def _():
        gather_inputs()

    @pl.when(s >= 2)
    def _():
        take_gates()

    @pl.when(s > 0)
    def _():
        prepare_hidden()

    def take_ret():
        remote(ret, gi, ss_ret.at[0], rs_ret.at[0], section=below).wait_recv()

    @pl.when(s == SECTIONS - 1)
    def _():
        take_ret()
        gather_inputs()

    @pl.when(s > 0)
    def _():
        prepare_inputs()

    def spread(m):
        for k in range(1, DP):
            j = peer(k)
            remote(backs.at[m, r], backs.at[m, j], ss_b.at[m, k], rs_b.at[m, j], dp=j).wait_recv()
        for k in range(DP):
            rows = slice(k * ROWS, (k + 1) * ROWS)
            back = backs[m, k].astype(F32)
            gate = gates[k, m].astype(F32)
            sigma = jax.nn.sigmoid(gate)
            dga[m, rows, :] = (
                back * ups[k, m].astype(F32) * sigma * (1.0 + gate * (1.0 - sigma))
            ).astype(BF16)
            dua[m, rows, :] = (back * gate * sigma).astype(BF16)

    spread(0)
    for m in range(MICRO):
        for k in range(1, DP):
            j = peer(k)
            remote(
                dyg.at[m, pl.ds(0, 2)], dys.at[m, j], ss_dy.at[m, k], rs_dy.at[m, j], dp=j
            ).wait_recv()
    for i in range(HID // 256):
        rows = slice(i * 256, (i + 1) * 256)
        for h in range(2):
            value = dot(hid_t[rows, :ALL], dys[0, :, h].reshape(ALL, CB))
            value = value + dot(hid_t[rows, ALL:], dys[1, :, h].reshape(ALL, CB))
            gd[rows, h * CB : (h + 1) * CB] = value.astype(BF16)

    @pl.when(s == 0)
    def _():
        for m in range(MICRO):
            for offset in OFFSETS:
                j = near(n, offset)
                for half in range(2):
                    remote(
                        fs.at[m, 0, half], fr.at[m, j, half], ss_f.at[m, 0, half],
                        rs_f.at[m, j, half], node=j,
                    ).wait_recv()
        for half in range(2):
            totals = []
            for m in range(MICRO):
                total = fr[m, 0, half].astype(F32)
                for j in range(1, NODES):
                    total = total + fr[m, j, half].astype(F32)
                totals.append(total)
            for c in range(2):
                start = half * HALF + c * 2 * CB
                gi[:, start : start + 2 * CB] = jnp.concatenate(
                    [total[c * OWN : (c + 1) * OWN] for total in totals], axis=0
                ).astype(BF16)

    @pl.when(jnp.logical_and(s > 0, s < SECTIONS - 1))
    def _():
        take_ret()

    grad_in[...] = gi[...]
    spread(1)

    @pl.when(s == SECTIONS - 1)
    def _():
        for q in range(NODES - 1):
            send_go(q, 0).wait_send()

    @pl.when(s == 1)
    def _():
        for q in range(NODES - 1):
            send_go(q, 1).wait_send()

    for k in range(1, DP):
        if k != 2:
            send_gate(k).wait_send()
            send_up(k).wait_send()
        send_lx(k).wait_send()
        send_cr(k).wait_send()
    for q in range(NODES - 1):
        send_lg(q).wait_send()
    for which in range(2):
        for half in range(2):
            forward(which, half).wait_send()
    for m in range(MICRO):
        for k in range(1, DP):
            send_b(m, k).wait_send()
            send_dy(m, k).wait_send()

    @pl.when(s < SECTIONS - 1)
    def _():
        for m in range(MICRO):
            for q in range(NODES - 1):
                send_ga(m, q).wait_send()
        send_ret().wait_send()

    @pl.when(s > 0)
    def _():
        for m in range(MICRO):
            for j in range(NODES):
                send_sc(m, j).wait_send()

    @pl.when(s == 0)
    def _():
        for m in range(MICRO):
            for q in range(NODES - 1):
                for step in range(2):
                    send_f(m, q, step).wait_send()


def finish(
    grad_in, lin, dg, du, down,
    o_in, o_gate, o_up, o_down,
    gate_v, up_v, sems,
):
    stores = [
        pltpu.make_async_copy(down, o_down, sems.at[0]),
        pltpu.make_async_copy(grad_in, o_in, sems.at[1]),
    ]
    for copy in stores:
        copy.start()
    for which, (d, staged, out) in enumerate(((dg, gate_v, o_gate), (du, up_v, o_up))):
        for i in range(DB // 256):
            rows = pl.ds(i * 256, 256)
            value = dot(lin[rows, :ALL], d[0]) + dot(lin[rows, ALL:], d[1])
            staged[rows, :] = value.astype(BF16)
            stores.append(
                pltpu.make_async_copy(
                    staged.at[rows, :], out.at[rows, :], sems.at[2 + 3 * which + i]
                )
            )
            stores[-1].start()
    for copy in stores:
        copy.wait()


def shards(grad_out, layer_in, gate_pre, up_pre, expert_ids, route_weight, w_gate, w_up, w_down):
    both = MICRO * OWN
    dma = pltpu.SemaphoreType.DMA
    vmem = pltpu.VMEM
    scratch = [
        vmem((NODES, HID // NODES, WIDTH), BF16),
        vmem((RING, CB, HID), BF16),
        vmem((NODES, CB, HID), BF16),
        vmem((NODES, 2 * HID, CB), BF16),
        vmem((MICRO, 2, ROWS), jnp.int32),
        vmem((MICRO, 2, ROWS), F32),
        vmem((both, WIDTH), BF16),
        vmem((MICRO * ROWS, 1), F32),
        vmem((MICRO, ROWS, 2 * HID), F32),
        vmem((NODES, 2, both, HALF), BF16),
        vmem((MICRO, NODES, ROWS, CB), BF16),
        vmem((MICRO, NODES, ROWS, CB), BF16),
        vmem((MICRO, NODES, ROWS, CB), BF16),
        vmem((MICRO, ROWS, 2 * HID), BF16),
        vmem((DP, MICRO, ROWS, HID), BF16),
        vmem((DP, MICRO, ROWS, HID), BF16),
        vmem((MICRO, DP, ROWS, HID), BF16),
        vmem((MICRO, DP, 2, ROWS, CB), BF16),
        vmem((DP, 8, MICRO * ROWS), F32),
        vmem((DP, both, DB), BF16),
        vmem((DP, both, DB), BF16),
        vmem((NODES, DP, both, DB), BF16),
        vmem((HID, MICRO * ALL), BF16),
        vmem((both, WIDTH), BF16),
        vmem((both, WIDTH), BF16),
        vmem((NODES, NODES, OWN, CB), F32),
        vmem((MICRO, NODES - 1, 2, 16, 2 * CB), BF16),
        vmem((MICRO, NODES, 2, 16, 2 * CB), BF16),
        dma((8,)),
        dma((NODES,)),
        dma((2 * NODES,)),
        dma((NODES,)),
        dma((NODES, 2)),
        dma((MICRO, NODES)),
        dma((MICRO, NODES)),
        dma((MICRO, NODES)),
        dma((MICRO, NODES)),
        dma((DP,)),
        dma((DP,)),
        dma((DP,)),
        dma((DP,)),
        dma((DP,)),
        dma((DP,)),
        dma((NODES,)),
        dma((NODES,)),
        dma((4,)),
        dma((4,)),
        dma((DP,)),
        dma((DP,)),
        dma((MICRO, DP)),
        dma((MICRO, DP)),
        dma((MICRO, DP)),
        dma((MICRO, DP)),
        dma((1,)),
        dma((1,)),
        dma((MICRO, NODES, 2)),
        dma((MICRO, NODES, 2)),
    ]
    anywhere = pl.BlockSpec(memory_space=pl.ANY)
    inside = pl.BlockSpec(memory_space=pltpu.VMEM)
    left = pl.pallas_call(
        body,
        out_shape=(
            vmem((both, WIDTH), BF16),
            vmem((DB, MICRO * ALL), BF16),
            vmem((MICRO, ALL, HID), BF16),
            vmem((MICRO, ALL, HID), BF16),
            vmem((HID, DB), BF16),
        ),
        in_specs=[anywhere] * 9,
        out_specs=(inside,) * 5,
        scratch_shapes=scratch,
        compiler_params=pltpu.CompilerParams(
            collective_id=0, has_side_effects=True, vmem_limit_bytes=53 * 2**20
        ),
        cost_estimate=pl.CostEstimate(flops=5 * 10**9, bytes_accessed=24 * 10**6, transcendentals=10**6),
        name="relay",
    )(
        grad_out.reshape(both, WIDTH),
        layer_in.reshape(both, WIDTH),
        gate_pre[0],
        up_pre[0],
        expert_ids[0].transpose(0, 2, 1),
        route_weight[0].transpose(0, 2, 1),
        w_gate[0],
        w_up[0],
        w_down[0],
    )
    grad_in, g_gate, g_up, g_down = pl.pallas_call(
        finish,
        out_shape=(
            jax.ShapeDtypeStruct((both, WIDTH), BF16),
            jax.ShapeDtypeStruct((DB, HID), BF16),
            jax.ShapeDtypeStruct((DB, HID), BF16),
            jax.ShapeDtypeStruct((HID, DB), BF16),
        ),
        in_specs=[inside] * 5,
        out_specs=(anywhere,) * 4,
        scratch_shapes=[
            vmem((DB, HID), BF16),
            vmem((DB, HID), BF16),
            dma((8,)),
        ],
        compiler_params=pltpu.CompilerParams(vmem_limit_bytes=30 * 2**20),
        cost_estimate=pl.CostEstimate(flops=16 * 10**8, bytes_accessed=10**7, transcendentals=0),
        name="finish",
    )(*(pltpu.with_memory_space_constraint(x, pltpu.VMEM) for x in left))
    return grad_in.reshape(1, MICRO, OWN, WIDTH), g_gate[None], g_up[None], g_down[None]


def solution(mesh):
    return jax.shard_map(
        shards,
        mesh=mesh,
        in_specs=(
            P(None, ("dp", "node"), None),
            P("section", None, ("dp", "node"), None),
            P("section", None, "dp", "node"),
            P("section", None, "dp", "node"),
            P("section", None, "dp", None),
            P("section", None, "dp", None),
            P("section", None, "node"),
            P("section", None, "node"),
            P("section", "node", None),
        ),
        out_specs=(
            P("section", None, ("dp", "node"), None),
            P("section", "dp", "node"),
            P("section", "dp", "node"),
            P("section", "node", "dp"),
        ),
        check_vma=False,
    )
```
